128 devices in a mesh: rows: 4 (over x_lo, core), cols: 32 (over x_hi, y, z).
Axes of the slice: x: 4 (x_hi: 2, x_lo: 2; x = x_hi * 2 + x_lo), y: 4, z: 4, core: 2. Of those that a mesh axis runs over, the one named last changes fastest.
Arguments:
- atm_flux: bfloat16 [8192, 32, 128], P(('rows', 'cols')), may hold values from -6 to 6
- remap_weights: bfloat16 [64, 3, 128, 4096], P('rows', None, None, 'cols'), may hold values from -0.3125 to 0.3125
- intersection: int32 [64, 32, 3], P('rows', 'cols'), may hold values from 0 to 8191, as said below
- tracers: float32 [2, 62, 64, 4096], P(None, None, 'rows', 'cols'), may hold values from -6 to 6
- east_speed: float32 [62, 64, 4096], P(None, 'rows', 'cols'), may hold values from -0.25 to 0.25
- north_speed: float32 [62, 64, 4096], P(None, 'rows', 'cols'), may hold values from -0.25 to 0.25
- mixing: float32 [62, 64, 4096], P(None, 'rows', 'cols'), may hold values from 0.05 to 20
- level_count: int32 [64, 4096], P('rows', 'cols'), may hold values from 0 to 62
Outputs:
- ocean_flux: float32 [32, 64, 4096], P(None, 'rows', 'cols')
- tracers_out: float32 [2, 62, 64, 4096], P(None, None, 'rows', 'cols')
The draws below stay inside these ranges and needn't reach their ends.
Inputs may be any that keep to these rules, and one draw needn't show every extreme that they name: `intersection`: slot s of ocean row y in longitude tile c names an atmosphere block held by the device of row group y // 16 and column index (c + 16 + s - 1) mod 32, blocks numbered device by device in the mesh order.
All inputs are finite; a program needn't handle non-finite values.
Results may differ from the reference program's by a relative error of at most 0.00075.
Values may be sent and summed in bfloat16 or wider, within the bound.
No kernel may reach another device: no remote copies, remote signals or barrier semaphores. Data moves between devices by JAX's collectives and lax.ppermute only.
A program may use at most 128 MiB of HBM per device.

```python
import math
import jax
import jax.numpy as jnp
from jax import lax

FIELDS = 32
ATM_CELLS = 128
LON_CELLS = 128
LEVELS = 62
SLOTS = 3
STEPS = 2
LAT_ROWS = 16
ATM_BLOCKS = 64
LON_TILES = 32
LON_OFFSET = 16
NY = 64
NX = 4096
ATM_TOTAL = 8192


def draw_intersection(key, part):
    row_group = jnp.arange(NY, dtype=jnp.int32) // LAT_ROWS
    tile = jnp.arange(LON_TILES, dtype=jnp.int32)
    slot_index = jnp.arange(SLOTS, dtype=jnp.int32)
    column = (tile[None, :, None] + LON_OFFSET + slot_index[None, None, :] - 1) % LON_TILES
    device = row_group[:, None, None] * LON_TILES + column
    within = jax.random.randint(key, (NY, LON_TILES, SLOTS), 0, ATM_BLOCKS)
    return (device * ATM_BLOCKS + within).astype(jnp.int32)


def with_ends(result, stream_key, low, largest):
    index_at = [jax.random.randint(jax.random.fold_in(stream_key, axis), (), 0, length) for axis, length in enumerate(result.shape)]
    main_axis = result.shape.index(max(result.shape))
    beside = index_at[:main_axis] + [(index_at[main_axis] + 1) % result.shape[main_axis]] + index_at[main_axis + 1:]
    return result.at[tuple(index_at)].set(low).at[tuple(beside)].set(largest)


def block_levels(rng, extent, shards, least, high):
    level, own = 1.0, jax.random.fold_in(rng, 6)
    for dim, parts in shards:
        heights = jnp.exp(jax.random.uniform(jax.random.fold_in(own, dim), (parts,), jnp.float32, least / len(shards), high / len(shards)))
        level = level * jnp.repeat(heights, extent[dim] // parts).reshape([-1 if axis == dim else 1 for axis in range(len(extent))])
    return level


def scatter_about(key, shape, scale, reach, cuts=(), kind=jnp.bfloat16):
    values = scale * jax.random.normal(key, shape, jnp.float32)
    if cuts:
        values = values * block_levels(key, shape, cuts, -0.22, 0.18)
    return jnp.clip(values, -reach, reach).astype(kind)


def setup_inputs(seed: int = 0) -> dict:
    streams_of = jax.random.split(jax.random.key(seed), 9)
    return {
        "atm_flux": scatter_about(streams_of[0], (ATM_TOTAL, FIELDS, ATM_CELLS), 1.0, 6.0, ((0, 128),)),
        "remap_weights": scatter_about(streams_of[1], (NY, SLOTS, ATM_CELLS, NX), (SLOTS * ATM_CELLS) ** -0.5, 0.3125, ((0, 4), (3, 32))),
        "intersection": draw_intersection(jax.random.fold_in(streams_of[8], 71), 0),
        "tracers": scatter_about(streams_of[3], (2, LEVELS, NY, NX), 1.0, 6.0, ((2, 4), (3, 32)), jnp.float32),
        "east_speed": jnp.clip(jax.random.uniform(streams_of[4], (LEVELS, NY, NX), jnp.float32, -0.25, 0.25) * block_levels(streams_of[4], (LEVELS, NY, NX), ((1, 4), (2, 32)), -0.4, 0.0), -0.25, 0.25),
        "north_speed": jnp.clip(jax.random.uniform(streams_of[5], (LEVELS, NY, NX), jnp.float32, -0.25, 0.25) * block_levels(streams_of[5], (LEVELS, NY, NX), ((1, 4), (2, 32)), -0.4, 0.0), -0.25, 0.25),
        "mixing": jnp.clip(jnp.exp(math.log(20.0) - 5.9914645 * jax.random.uniform(streams_of[6], (LEVELS, NY, NX), jnp.float32) ** block_levels(streams_of[6], (LEVELS, NY, NX), ((1, 4), (2, 32)), -0.2, 0.2)), 0.05, 20.0),
        "level_count": with_ends(jax.random.randint(streams_of[7], (NY, NX), 0, LEVELS + 1), jax.random.fold_in(streams_of[7], 1), 0, LEVELS).astype(jnp.int32),
    }


def advect(field, east_speed, north_speed, wet_mask):
    east_face = east_speed[:, :, :-1] * jnp.where(east_speed[:, :, :-1] > 0, field[..., :-1], field[..., 1:]) * (wet_mask[:, :, :-1] * wet_mask[:, :, 1:])
    north_face = north_speed[:, :-1, :] * jnp.where(north_speed[:, :-1, :] > 0, field[..., :-1, :], field[..., 1:, :]) * (wet_mask[:, :-1, :] * wet_mask[:, 1:, :])
    across = (east_face[..., 1:] - east_face[..., :-1])[..., 1:-1, :]
    along = (north_face[..., 1:, :] - north_face[..., :-1, :])[..., :, 1:-1]
    return field[..., 1:-1, 1:-1] - across - along


def vertical_mix(field, mixing, wet_mask):
    count = field.shape[1]
    below = jnp.concatenate([wet_mask[1:], jnp.zeros_like(wet_mask[:1])], 0)
    upper = mixing * wet_mask * below
    ratios = []
    values = []
    ratio_prev = jnp.zeros(upper.shape[1:], jnp.float32)
    value_prev = jnp.zeros(field[:, 0].shape, jnp.float32)
    for level in range(count):
        up_k = upper[level]
        if level > 0:
            low_k = upper[level - 1]
            denom = 1.0 + low_k + up_k + low_k * ratio_prev
            value_now = (field[:, level] + low_k * value_prev) / denom
        else:
            denom = 1.0 + up_k
            value_now = field[:, level] / denom
        ratio_now = -up_k / denom
        ratios.append(ratio_now)
        values.append(value_now)
        ratio_prev = ratio_now
        value_prev = value_now
    solved = [None] * count
    next_value = values[count - 1]
    solved[count - 1] = next_value
    for level in range(count - 2, -1, -1):
        next_value = values[level] - ratios[level] * next_value
        solved[level] = next_value
    return jnp.stack(solved, 1)


def pad_global(array):
    widths = [(0, 0)] * (array.ndim - 2) + [(1, 1), (0, 0)]
    padded = jnp.pad(array, widths)
    return jnp.concatenate([padded[..., -1:], padded, padded[..., :1]], axis=-1)


def reference(atm_flux, remap_weights, intersection, tracers, east_speed, north_speed, mixing, level_count):
    def one_row(items):
        row_intersection, row_weights = items
        blocks = atm_flux[row_intersection].astype(jnp.float32)
        weights = row_weights.reshape(SLOTS, ATM_CELLS, LON_TILES, LON_CELLS).astype(jnp.float32)
        return jnp.einsum("csfa,sact->fct", blocks, weights).reshape(FIELDS, NX)

    rows_out = lax.map(one_row, (intersection, remap_weights))
    ocean_flux = jnp.transpose(rows_out, (1, 0, 2))
    levels = lax.broadcasted_iota(jnp.int32, (LEVELS, NY, NX), 0)
    wet_mask = (levels < level_count[None]).astype(jnp.float32)
    field = tracers.at[:, 0].add(0.5 * ocean_flux[:2] * wet_mask[0])
    east_pad = pad_global(east_speed)
    north_pad = pad_global(north_speed)
    wet_pad = pad_global(wet_mask)
    for step_index in range(STEPS):
        field = advect(pad_global(field), east_pad, north_pad, wet_pad)
        field = vertical_mix(field, mixing, wet_mask)
    return ocean_flux, field
```

```python
import jax
import jax.numpy as jnp
from jax import lax
from jax.experimental import pallas as pl
from jax.experimental.pallas import tpu as pltpu
from jax.sharding import PartitionSpec as P

F32 = jnp.float32
BF16 = jnp.bfloat16
VMEM = pl.BlockSpec(memory_space=pltpu.VMEM)
SMEM = pl.BlockSpec(memory_space=pltpu.SMEM)
INTERPRET = False
LIMIT = 24 * 1024 * 1024


def lanes(shape):
    return lax.broadcasted_iota(jnp.int32, shape, len(shape) - 1)


def sublanes(shape):
    return lax.broadcasted_iota(jnp.int32, shape, len(shape) - 2)


def turn(x, shift):
    shift = shift % x.shape[-1]
    return x if shift == 0 else pltpu.roll(x, shift, x.ndim - 1)


def prepare_kernel(
    tracers, east, north, mixing, count,
    face_e, face_n, inv, low, ratio, first, go_e, go_w, go_n, go_s,
):
    levels, height, width = east.shape
    lane, row = lanes((height, width)), sublanes((height, width))
    depth = count[...]
    zero = jnp.zeros((height, width), F32)
    a_prev, r_prev, low_a = zero, zero, zero
    e_x, w_x, e_c = zero, zero, zero
    for k in range(levels):
        wet = jnp.where(depth > k, 1.0, 0.0)
        wet_e = jnp.where(lane == width - 1, 1.0, turn(wet, -1))
        wet_n = jnp.where(row == height - 1, 1.0, pltpu.roll(wet, height - 1, 0))
        ce = east[k] * wet * wet_e
        face_e[k] = ce
        cn = north[k] * wet * wet_n
        face_n[k] = cn
        go_n[2, k : k + 1, :] = cn[height - 1 :, :]
        e_c = jnp.where(lane == k, turn(ce, k - (width - 1)), e_c)
        for t in range(2):
            x = tracers[t, k]
            at = k + t * (width // 2)
            e_x = jnp.where(lane == at, turn(x, at - (width - 1)), e_x)
            w_x = jnp.where(lane == at, turn(x, at), w_x)
            go_n[t, k : k + 1, :] = x[height - 1 :, :]
            go_s[t, k : k + 1, :] = x[:1, :]
        a = mixing[k] * jnp.where(depth > k + 1, 1.0, 0.0) if k + 1 < levels else zero
        iv = 1.0 / (1.0 + a_prev + a - a_prev * r_prev)
        inv[k] = iv
        low[k] = a_prev * iv
        r_prev = a * iv
        ratio[k] = r_prev
        a_prev = a
    for t in range(2):
        first[t] = tracers[t, 0]
    spare = go_n.shape[1] - levels
    for t in range(3):
        go_n[t, levels:, :] = jnp.zeros((spare, width), F32)
        go_s[t, levels:, :] = jnp.zeros((spare, width), F32)
    go_e[0], go_w[0], go_e[1] = e_x, w_x, e_c
    go_w[1] = jnp.where(lane < depth[:, :1], 1.0, 0.0)
    tall = sublanes((go_s.shape[1], width))
    go_s[2] = jnp.where(tall < depth[:1, :], 1.0, 0.0)


def force_kernel(
    place, index, a0, a1, a2, weights, count, first, go_e, go_w, go_n, go_s,
    forced, out_c0, out_c1, out_r0, out_r1, held, picked,
):
    height, width = count.shape
    blocks = a0.shape[0] // 2
    for s, a in enumerate((a0, a1, a2)):
        held[s] = a[...].astype(F32)
    for y in range(height):
        for s in range(3):
            b = lax.rem(index[3 * y + s], blocks)
            for f in range(2):
                picked[8 * y + f : 8 * y + f + 1, s * 128 : (s + 1) * 128] = held[
                    s, pl.ds(b + f * blocks, 1), :
                ]
    wet = jnp.where(count[...] > 0, 0.5, 0.0)
    for y in range(height):
        got = jnp.dot(
            picked[8 * y : 8 * y + 8].astype(BF16), weights[y], preferred_element_type=F32
        )
        for f in range(2):
            forced[f, y : y + 1, :] = got[f : f + 1, :]
    lane = lanes((height, width))
    e_x, w_x = go_e[0], go_w[0]
    tops, bottoms = [], []
    for t in range(2):
        x = first[t] + wet * forced[t]
        forced[t] = x
        at = t * (width // 2)
        e_x = jnp.where(lane == at, turn(x, at - (width - 1)), e_x)
        w_x = jnp.where(lane == at, turn(x, at), w_x)
        tops.append(x[height - 1 :, :])
        bottoms.append(x[:1, :])
    even_r, even_c = place[0] == 0, place[1] == 0
    out_c0[0] = jnp.where(even_c, e_x, w_x)
    out_c1[0] = jnp.where(even_c, w_x, e_x)
    out_c0[1] = jnp.where(even_c, go_e[1], go_w[1])
    out_c1[1] = jnp.where(even_c, go_w[1], go_e[1])
    out_r0[...] = jnp.where(even_r, go_n[...], go_s[...])
    out_r1[...] = jnp.where(even_r, go_s[...], go_n[...])
    for t in range(2):
        out_r0[t, :1, :] = jnp.where(even_r, tops[t], bottoms[t])
        out_r1[t, :1, :] = jnp.where(even_r, bottoms[t], tops[t])


def step(place, field, level0, face_e, face_n, inv, low, ratio, count,
         c0, c1, r0, r1, s0, s1, q0, q1, solved, out, messages):
    levels, height, width = face_e.shape
    lane, row = lanes((height, width)), sublanes((height, width))
    depth = count[...]
    even_r, even_c = place[0] == 0, place[1] == 0
    x_e = jnp.where(even_c, c0, c1)
    x_w = jnp.where(even_c, c1, c0)
    k_e = jnp.where(even_c, s0, s1)
    k_w = jnp.where(even_c, s1, s0)
    east_end, west_end = lane == width - 1, lane == 0
    north_end, south_end = row == height - 1, row == 0
    value = [None, None]
    for k in range(levels):
        wet = jnp.where(depth > k, 1.0, 0.0)
        ce = face_e[k]
        ce = jnp.where(east_end, ce * turn(k_e, width - 1 - k), ce)
        cw = turn(k_w, -k) * wet
        pa, pb = q0[k : k + 1, :], q1[k : k + 1, :]
        cn = face_n[k]
        cn = jnp.where(north_end, cn * jnp.where(even_r, pa, pb), cn)
        cs = jnp.where(even_r, pb, pa) * wet
        for t in range(2):
            x = level0[t] if (k == 0 and level0 is not None) else field[t, k]
            at = k + t * (width // 2)
            right = jnp.where(east_end, turn(x_e, width - 1 - at), turn(x, -1))
            fe = ce * jnp.where(ce > 0, x, right)
            fw = cw * jnp.where(cw > 0, turn(x_w, -at), x)
            fw = jnp.where(west_end, fw, turn(fe, 1))
            ra, rb = r0[t, k : k + 1, :], r1[t, k : k + 1, :]
            above = jnp.where(north_end, jnp.where(even_r, ra, rb), pltpu.roll(x, height - 1, 0))
            fn = cn * jnp.where(cn > 0, x, above)
            fs = cs * jnp.where(cs > 0, jnp.where(even_r, rb, ra), x)
            fs = jnp.where(south_end, fs, pltpu.roll(fn, 1, 0))
            moved = x - (fe - fw) - (fn - fs)
            now = moved * inv[k]
            if k:
                now = now + low[k] * value[t]
            value[t] = now
            solved[t, k] = now
    zero = jnp.zeros((height, width), F32)
    e_x, w_x = zero, zero
    for k in range(levels - 1, -1, -1):
        for t in range(2):
            if k < levels - 1:
                value[t] = solved[t, k] + ratio[k] * value[t]
            y = value[t]
            out[t, k] = y
            if messages is not None:
                at = k + t * (width // 2)
                e_x = jnp.where(lane == at, turn(y, at - (width - 1)), e_x)
                w_x = jnp.where(lane == at, turn(y, at), w_x)
                top, bottom = y[height - 1 :, :], y[:1, :]
                messages[2][t, k : k + 1, :] = jnp.where(even_r, top, bottom)
                messages[3][t, k : k + 1, :] = jnp.where(even_r, bottom, top)
    if messages is not None:
        messages[0][...] = jnp.where(even_c, e_x, w_x)
        messages[1][...] = jnp.where(even_c, w_x, e_x)
        spare = messages[2].shape[1] - levels
        for t in range(2):
            messages[2][t, levels:, :] = jnp.zeros((spare, width), F32)
            messages[3][t, levels:, :] = jnp.zeros((spare, width), F32)


def first_step_kernel(
    place, tracers, forced, face_e, face_n, inv, low, ratio, count, c0, c1, r0, r1,
    out, out_c0, out_c1, out_r0, out_r1, solved,
):
    step(place, tracers, forced, face_e, face_n, inv, low, ratio, count,
         c0[0], c1[0], r0, r1, c0[1], c1[1], r0.at[2], r1.at[2], solved, out,
         (out_c0, out_c1, out_r0, out_r1))


def second_step_kernel(
    place, field, face_e, face_n, inv, low, ratio, count, c0, c1, r0, r1, p0, p1, u0, u1, out, solved,
):
    step(place, field, None, face_e, face_n, inv, low, ratio, count,
         p0[...], p1[...], u0, u1, c0[1], c1[1], r0.at[2], r1.at[2], solved, out, None)


def remap_kernel(index, a0, a1, a2, weights, out):
    blocks = a0.shape[0]
    for y in range(out.shape[1]):
        rows = []
        for s, a in enumerate((a0, a1, a2)):
            b = lax.rem(index[3 * y + s], blocks)
            rows.append(a[pl.ds(b, 1)][0])
        got = jnp.dot(jnp.concatenate(rows, 1), weights[y], preferred_element_type=F32)
        out[:, y, :] = got


def call(kernel, outs, specs, scratch=(), flops=0, **kw):
    return pl.pallas_call(
        kernel,
        out_shape=outs,
        in_specs=specs,
        out_specs=[VMEM] * len(outs),
        scratch_shapes=list(scratch),
        compiler_params=pltpu.CompilerParams(vmem_limit_bytes=LIMIT),
        interpret=INTERPRET,
        **kw,
    )


def swap(block, axis, pairs):
    return lax.ppermute(block, axis, [(a, b) for a, b in pairs] + [(b, a) for a, b in pairs])


def per_device(
    atm_flux, remap_weights, intersection, tracers, east_speed, north_speed, mixing, level_count
):
    tiles, groups = lax.axis_size("cols"), lax.axis_size("rows")
    levels, height, width = east_speed.shape
    tall = -(-levels // 8) * 8
    sds = lambda *shape, dtype=F32: jax.ShapeDtypeStruct(shape, dtype)

    def from_ahead(block, distance):
        return lax.ppermute(block, "cols", [((i + distance) % tiles, i) for i in range(tiles)])

    cols0 = [(i, i + 1) for i in range(0, tiles, 2)]
    cols1 = [(i, (i + 1) % tiles) for i in range(1, tiles, 2)]
    rows0 = [(i, i + 1) for i in range(0, groups - 1, 2)]
    rows1 = [(i, i + 1) for i in range(1, groups - 1, 2)]

    place = jnp.stack([lax.axis_index("rows") % 2, lax.axis_index("cols") % 2]).astype(jnp.int32)
    index = intersection.reshape(-1)
    weights = remap_weights.reshape(height, -1, width)

    few = jnp.concatenate([atm_flux[:, 0, :], atm_flux[:, 1, :]], 0)
    slots = [tiles // 2 + s - 1 for s in range(3)]
    part = [from_ahead(few, d) for d in slots]
    whole = [from_ahead(atm_flux, d) for d in slots]

    plane = sds(levels, height, width)
    face_e, face_n, inv, low, ratio, first, go_e, go_w, go_n, go_s = call(
        prepare_kernel,
        [plane] * 5
        + [sds(2, height, width)] * 3
        + [sds(3, tall, width)] * 2,
        [VMEM] * 5,
    )(tracers, east_speed, north_speed, mixing, level_count)

    forced, c0, c1, r0, r1 = call(
        force_kernel,
        [sds(2, height, width)] * 3 + [sds(3, tall, width)] * 2,
        [SMEM, SMEM] + [VMEM] * 10,
        [
            pltpu.VMEM((3, 2 * atm_flux.shape[0], width), F32),
            pltpu.VMEM((8 * height, 3 * width), F32),
        ],
    )(place, index, *part, weights, level_count, first, go_e, go_w, go_n, go_s)

    def exchange(c0, c1, r0, r1):
        g0, g1 = swap(r0, "rows", rows0), swap(r1, "rows", rows1)
        return swap(c0, "cols", cols0), swap(c1, "cols", cols1), g0, g1

    c0, c1, r0, r1 = exchange(c0, c1, r0, r1)
    coefficients = (face_e, face_n, inv, low, ratio, level_count)
    field, p0, p1, u0, u1 = call(
        first_step_kernel,
        [sds(2, levels, height, width)] + [sds(height, width)] * 2 + [sds(2, tall, width)] * 2,
        [SMEM] + [VMEM] * 12,
        [pltpu.VMEM((2, levels, height, width), F32)],
    )(place, tracers, forced, *coefficients, c0, c1, r0, r1)
    p0, p1, u0, u1 = exchange(p0, p1, u0, u1)
    (result,) = call(
        second_step_kernel,
        [sds(2, levels, height, width)],
        [SMEM] + [VMEM] * 15,
        [pltpu.VMEM((2, levels, height, width), F32)],
    )(place, field, *coefficients, c0, c1, r0, r1, p0, p1, u0, u1)
    (ocean_flux,) = call(
        remap_kernel,
        [sds(atm_flux.shape[1], height, width)],
        [SMEM] + [VMEM] * 4,
    )(index, *whole, weights)
    return (ocean_flux, result)


def solution(mesh):
    placed = (
        P(("rows", "cols"), None, None),
        P("rows", None, None, "cols"),
        P("rows", "cols", None),
        P(None, None, "rows", "cols"),
        P(None, "rows", "cols"),
        P(None, "rows", "cols"),
        P(None, "rows", "cols"),
        P("rows", "cols"),
    )
    return jax.shard_map(
        per_device,
        mesh=mesh,
        in_specs=placed,
        out_specs=(P(None, "rows", "cols"), P(None, None, "rows", "cols")),
        check_vma=False,
    )
```

```python
import jax
import jax.numpy as jnp
from jax import lax
from jax.experimental import pallas as pl
from jax.experimental.pallas import tpu as pltpu
from jax.sharding import PartitionSpec as P

F32 = jnp.float32
BF16 = jnp.bfloat16
VMEM = pl.BlockSpec(memory_space=pltpu.VMEM)
ANY = pl.BlockSpec(memory_space=pl.ANY)
SMEM = pl.BlockSpec(memory_space=pltpu.SMEM)
LIMIT = 24 * 1024 * 1024


def lanes(shape):
    return lax.broadcasted_iota(jnp.int32, shape, len(shape) - 1)


def sublanes(shape):
    return lax.broadcasted_iota(jnp.int32, shape, len(shape) - 2)


def turn(x, shift):
    shift = shift % x.shape[-1]
    return x if shift == 0 else pltpu.roll(x, shift, x.ndim - 1)


def pack_kernel(tracers, east, north, count, first, tile, tops, bottoms):
    levels, height, width = east.shape
    lane = lanes((height, width))
    depth = count[...]
    packed = [jnp.zeros((height, width), F32) for _ in range(3)]
    for k in range(levels):
        here = (lane >> 1) == k
        for t in range(2):
            x = tracers[t, k]
            packed[t] = jnp.where(here, turn(x, 2 * k + 1), packed[t])
            tops[t, k : k + 1, :] = x[height - 1 :, :]
            bottoms[t, k : k + 1, :] = x[:1, :]
        packed[2] = jnp.where(here, turn(east[k], 2 * k + 1), packed[2])
        tops[2, k : k + 1, :] = north[k, height - 1 :, :]
    for t in range(2):
        first[t] = tracers[t, 0]
        tile[t] = packed[t]
    spare = tops.shape[1] - levels
    for t in range(3):
        tops[t, levels:, :] = jnp.zeros((spare, width), F32)
    for t in range(2):
        bottoms[t, levels:, :] = jnp.zeros((spare, width), F32)
    even = (lane & 1) == 0
    wet_last = jnp.where((lane >> 1) < depth[:, width - 1 :], 1.0, 0.0)
    wet_first = jnp.where((lane >> 1) < depth[:, :1], 1.0, 0.0)
    tile[2] = jnp.where(even, packed[2] * wet_last, wet_first)
    tall = sublanes(tops.shape[1:])
    tops[2] = tops[2] * jnp.where(tall < depth[height - 1 :, :], 1.0, 0.0)
    bottoms[2] = jnp.where(tall < depth[:1, :], 1.0, 0.0)


def solver_kernel(after, east, north, mixing, count, face_e, face_w, face_n, face_s, inv, low, ratio):
    levels, height, width = east.shape
    lane, row = lanes((height, width)), sublanes((height, width))
    depth = count[...]
    depth_e = jnp.where(lane == width - 1, levels, turn(depth, -1))
    depth_n = jnp.where(row == height - 1, levels, pltpu.roll(depth, height - 1, 0))
    depth_e = jnp.minimum(depth, depth_e)
    depth_n = jnp.minimum(depth, depth_n)
    a_prev = r_prev = jnp.zeros((height, width), F32)
    for k in range(levels):
        ce = jnp.where(depth_e > k, east[k], 0.0)
        cn = jnp.where(depth_n > k, north[k], 0.0)
        face_e[k] = ce
        face_w[k] = turn(ce, 1)
        face_n[k] = cn
        face_s[k] = pltpu.roll(cn, 1, 0)
        a = jnp.where(depth > k + 1, mixing[k], 0.0) if k + 1 < levels else jnp.zeros((height, width), F32)
        iv = 1.0 / (1.0 + a_prev + a - a_prev * r_prev)
        inv[k] = iv
        low[k] = a_prev * iv
        r_prev = a * iv
        ratio[k] = r_prev
        a_prev = a


def force_kernel(
    place, index, a0, a1, a2, weights, count, first, tile, tops, bottoms,
    forced, sent, out_r0, out_r1, held, picked,
):
    height, width = count.shape
    blocks = held.shape[1] // 2
    for s, a in enumerate((a0, a1, a2)):
        held[s] = a[: 2 * blocks].astype(F32)
    for y in range(height):
        for s in range(3):
            b = lax.rem(index[3 * y + s], blocks)
            for f in range(2):
                picked[8 * y + f : 8 * y + f + 1, s * 128 : (s + 1) * 128] = held[
                    s, pl.ds(b + f * blocks, 1), :
                ]
    wet = jnp.where(count[...] > 0, 0.5, 0.0)
    for y in range(height):
        got = jnp.dot(
            picked[8 * y : 8 * y + 8].astype(BF16), weights[y], preferred_element_type=F32
        )
        for f in range(2):
            forced[f, y : y + 1, :] = got[f : f + 1, :]
    here = lanes((height, width)) < 2
    even = place[0] == 0
    out_r0[...] = jnp.where(even, tops[...], bottoms[...])
    out_r1[...] = jnp.where(even, bottoms[...], tops[...])
    sent[2] = tile[2]
    for t in range(2):
        x = first[t] + wet * forced[t]
        forced[t] = x
        sent[t] = jnp.where(here, turn(x, 1), tile[t])
        top, bottom = x[height - 1 :, :], x[:1, :]
        out_r0[t, :1, :] = jnp.where(even, top, bottom)
        out_r1[t, :1, :] = jnp.where(even, bottom, top)


def step(place, field, level0, face_e, face_w, face_n, face_s, inv, low, ratio,
         own_c, got_c, own_r, got_r, coef_c, coef_r, solved, edge_n, edge_s, out, messages):
    levels, height, width = face_e.shape
    lane, row = lanes((height, width)), sublanes((height, width))
    even_r, even_c = place[0] == 0, place[1] == 0
    even = (lane & 1) == 0

    def facing(own, pair):
        a, b = pair
        from_e, from_w = jnp.where(even_c, a, b), jnp.where(even_c, b, a)
        theirs = jnp.where(even, from_w, from_e)
        mine = jnp.where(even, turn(own, -1), turn(own, 1))
        return theirs, mine

    c_theirs, c_mine = facing(*coef_c)
    c = c_theirs * c_mine
    edges = []
    for t in range(2):
        theirs, mine = facing(own_c[t], (got_c[0][t], got_c[1][t]))
        flux = c * jnp.where((c > 0) == even, theirs, mine)
        edges.append(jnp.where(even, flux, turn(flux, -2)))

    def row_pair(a, b):
        return jnp.where(even_r, a, b), jnp.where(even_r, b, a)

    own_n, own_s = row_pair(coef_r[0][...], coef_r[1][...])
    from_n, from_s = row_pair(coef_r[2][...], coef_r[3][...])
    cn_row, cs_row = own_n * from_n, own_s * from_s
    for t in range(2):
        own_n, own_s = row_pair(own_r[0][t], own_r[1][t])
        from_n, from_s = row_pair(got_r[0][t], got_r[1][t])
        edge_n[t] = cn_row * jnp.where(cn_row > 0, own_n, from_n)
        edge_s[t] = cs_row * jnp.where(cs_row > 0, from_s, own_s)

    east_end, west_end = lane == width - 1, lane == 0
    north_end, south_end = row == height - 1, row == 0
    value = [None, None]
    for k in range(levels):
        ce, cw, cn, cs = face_e[k], face_w[k], face_n[k], face_s[k]
        for t in range(2):
            x = level0[t] if (k == 0 and level0 is not None) else field[t, k]
            edge = turn(edges[t], -2 * k)
            fe = jnp.where(east_end, edge, ce * jnp.where(ce > 0, x, turn(x, -1)))
            fw = jnp.where(west_end, edge, cw * jnp.where(cw > 0, turn(x, 1), x))
            fn = cn * jnp.where(cn > 0, x, pltpu.roll(x, height - 1, 0))
            fn = jnp.where(north_end, edge_n[t, k : k + 1, :], fn)
            fs = cs * jnp.where(cs > 0, pltpu.roll(x, 1, 0), x)
            fs = jnp.where(south_end, edge_s[t, k : k + 1, :], fs)
            now = (x - (fe - fw) - (fn - fs)) * inv[k]
            if k:
                now = now + low[k] * value[t]
            value[t] = now
            solved[t, k] = now
    packed = [jnp.zeros((height, width), F32)] * 2
    for k in range(levels - 1, -1, -1):
        for t in range(2):
            if k < levels - 1:
                value[t] = solved[t, k] + ratio[k] * value[t]
            y = value[t]
            out[t, k] = y
            if messages is not None:
                packed[t] = jnp.where((lane >> 1) == k, turn(y, 2 * k + 1), packed[t])
                top, bottom = y[height - 1 :, :], y[:1, :]
                messages[1][t, k : k + 1, :] = jnp.where(even_r, top, bottom)
                messages[2][t, k : k + 1, :] = jnp.where(even_r, bottom, top)
    if messages is not None:
        spare = messages[1].shape[1] - levels
        for t in range(2):
            messages[0][t] = packed[t]
            messages[1][t, levels:, :] = jnp.zeros((spare, width), F32)
            messages[2][t, levels:, :] = jnp.zeros((spare, width), F32)


def first_step_kernel(
    place, tracers, forced, face_e, face_w, face_n, face_s, inv, low, ratio,
    c, c0, c1, r0, r1, g0, g1, out, out_c, out_r0, out_r1, solved, edge_n, edge_s,
):
    step(place, tracers, forced, face_e, face_w, face_n, face_s, inv, low, ratio,
         c, (c0, c1), (r0, r1), (g0, g1), (c[2], (c0[2], c1[2])),
         (r0.at[2], r1.at[2], g0.at[2], g1.at[2]), solved, edge_n, edge_s, out, (out_c, out_r0, out_r1))


def second_step_kernel(
    place, field, face_e, face_w, face_n, face_s, inv, low, ratio,
    c, c0, c1, r0, r1, g0, g1, d, d0, d1, u0, u1, h0, h1, out, solved, edge_n, edge_s,
):
    step(place, field, None, face_e, face_w, face_n, face_s, inv, low, ratio,
         d, (d0, d1), (u0, u1), (h0, h1), (c[2], (c0[2], c1[2])),
         (r0.at[2], r1.at[2], g0.at[2], g1.at[2]), solved, edge_n, edge_s, out, None)


def gather_kernel(after, wanted, atm, out0, out1, out2):
    for s, out in enumerate((out0, out1, out2)):
        for y in range(out.shape[0]):
            out[y] = atm[wanted[s * out.shape[0] + y]]


def remap_kernel(a0, a1, a2, weights, out):
    for y in range(out.shape[1]):
        picked = jnp.concatenate([a0[y], a1[y], a2[y]], 1)
        out[:, y, :] = jnp.dot(picked, weights[y], preferred_element_type=F32)


def call(kernel, outs, specs, scratch=(), cost=1):
    return pl.pallas_call(
        kernel,
        out_shape=outs,
        in_specs=specs,
        out_specs=[VMEM] * len(outs),
        scratch_shapes=list(scratch),
        compiler_params=pltpu.CompilerParams(vmem_limit_bytes=LIMIT),
        cost_estimate=pl.CostEstimate(flops=0, bytes_accessed=cost * 3000000, transcendentals=0),
    )


def swap(block, axis, pairs):
    return lax.ppermute(block, axis, [(a, b) for a, b in pairs] + [(b, a) for a, b in pairs])


def per_device(
    atm_flux, remap_weights, intersection, tracers, east_speed, north_speed, mixing, level_count
):
    tiles, groups = lax.axis_size("cols"), lax.axis_size("rows")
    levels, height, width = east_speed.shape
    tall = -(-levels // 8) * 8
    sds = lambda *shape, dtype=F32: jax.ShapeDtypeStruct(shape, dtype)

    def from_ahead(block, distance):
        return lax.ppermute(block, "cols", [((i + distance) % tiles, i) for i in range(tiles)])

    cols0 = [(i, i + 1) for i in range(0, tiles, 2)]
    cols1 = [(i, (i + 1) % tiles) for i in range(1, tiles, 2)]
    rows0 = [(i, i + 1) for i in range(0, groups - 1, 2)]
    rows1 = [(i, i + 1) for i in range(1, groups - 1, 2)]

    place = jnp.stack([lax.axis_index("rows") % 2, lax.axis_index("cols") % 2]).astype(jnp.int32)
    weights = remap_weights.reshape(height, -1, width)

    blocks, fields = atm_flux.shape[:2]
    within = intersection[:, 0, :] % blocks
    asked = jnp.broadcast_to(within.T.reshape(-1, 1), (3 * height, width)).astype(BF16)
    few = jnp.concatenate([atm_flux[:, 0, :], atm_flux[:, 1, :], asked], 0)
    slots = [tiles // 2 + s - 1 for s in range(3)]
    part = [from_ahead(few, d) for d in slots]

    plane = sds(levels, height, width)
    first, tile, tops, bottoms = call(
        pack_kernel,
        [sds(2, height, width), sds(3, height, width)] + [sds(3, tall, width)] * 2,
        [VMEM] * 4,
        cost=2,
    )(tracers, east_speed, north_speed, level_count)

    forced, c, r0, r1 = call(
        force_kernel,
        [sds(2, height, width), sds(3, height, width)] + [sds(3, tall, width)] * 2,
        [SMEM, SMEM] + [VMEM] * 9,
        [pltpu.VMEM((3, 2 * blocks, width), F32), pltpu.VMEM((8 * height, 3 * width), F32)],
        cost=1,
    )(place, within.reshape(-1), *part, weights, level_count, first, tile, tops, bottoms)

    def exchange(c, r0, r1):
        g0, g1 = swap(r0, "rows", rows0), swap(r1, "rows", rows1)
        return swap(c, "cols", cols0), swap(c, "cols", cols1), g0, g1

    c0, c1, g0, g1 = exchange(c, r0, r1)
    coefficients = call(solver_kernel, [plane] * 7, [ANY] + [VMEM] * 4, cost=4)(
        g0, east_speed, north_speed, mixing, level_count
    )
    wanted = jnp.concatenate(
        [part[s][2 * blocks + (2 - s) * height :][:height, 0] for s in range(3)]
    ).astype(jnp.int32)
    found = call(
        gather_kernel,
        [sds(height, fields, width, dtype=BF16)] * 3,
        [ANY, SMEM, VMEM],
        cost=1,
    )(g1, wanted, atm_flux)
    blocks_of = [from_ahead(found[2 - s], slots[s]) for s in range(3)]

    scratch = [pltpu.VMEM((2, levels, height, width), F32)] + [pltpu.VMEM((2, tall, width), F32)] * 2
    field, d, u0, u1 = call(
        first_step_kernel,
        [sds(2, levels, height, width), sds(2, height, width)] + [sds(2, tall, width)] * 2,
        [SMEM] + [VMEM] * 16,
        scratch,
        cost=4,
    )(place, tracers, forced, *coefficients, c, c0, c1, r0, r1, g0, g1)
    d0, d1, h0, h1 = exchange(d, u0, u1)
    (ocean_flux,) = call(remap_kernel, [sds(fields, height, width)], [VMEM] * 4, cost=2)(
        *blocks_of, weights
    )
    (result,) = call(
        second_step_kernel,
        [sds(2, levels, height, width)],
        [SMEM] + [VMEM] * 22,
        scratch,
        cost=3,
    )(place, field, *coefficients, c, c0, c1, r0, r1, g0, g1, d, d0, d1, u0, u1, h0, h1)
    return (ocean_flux, result)


def solution(mesh):
    placed = (
        P(("rows", "cols"), None, None),
        P("rows", None, None, "cols"),
        P("rows", "cols", None),
        P(None, None, "rows", "cols"),
        P(None, "rows", "cols"),
        P(None, "rows", "cols"),
        P(None, "rows", "cols"),
        P("rows", "cols"),
    )
    return jax.shard_map(
        per_device,
        mesh=mesh,
        in_specs=placed,
        out_specs=(P(None, "rows", "cols"), P(None, None, "rows", "cols")),
        check_vma=False,
    )
```

```python
import jax
import jax.numpy as jnp
from jax import lax
from jax.experimental import pallas as pl
from jax.experimental.pallas import tpu as pltpu
from jax.sharding import PartitionSpec as P

F32 = jnp.float32
BF16 = jnp.bfloat16
VMEM = pl.BlockSpec(memory_space=pltpu.VMEM)
ANY = pl.BlockSpec(memory_space=pl.ANY)
SMEM = pl.BlockSpec(memory_space=pltpu.SMEM)
LIMIT = 24 * 1024 * 1024
FULL = 60 * 1024 * 1024


def lanes(shape):
    return lax.broadcasted_iota(jnp.int32, shape, len(shape) - 1)


def sublanes(shape):
    return lax.broadcasted_iota(jnp.int32, shape, len(shape) - 2)


def turn(x, shift):
    shift = shift % x.shape[-1]
    return x if shift == 0 else pltpu.roll(x, shift, x.ndim - 1)


def ask_kernel(index, atm, out, held, wide, sem):
    blocks = atm.shape[0]
    rows = held.shape[1]
    copy = pltpu.make_async_copy(atm.at[:, :rows, :], held, sem)
    copy.start()
    height = index.shape[0]
    for s in range(3):
        for y in range(height):
            at = 2 * blocks + s * height + y
            b = lax.rem(index[y, 0, s], blocks).astype(F32)
            wide[at : at + 1, :] = jnp.full((1, wide.shape[1]), b, F32)
    copy.wait()
    for b in range(blocks):
        x = held[b].astype(F32)
        for f in range(2):
            wide[b + f * blocks : b + f * blocks + 1, :] = x[f : f + 1, :]
    out[...] = wide[...].astype(BF16)


def pack_kernel(tracers, east, north, count, first, tile, tops, bottoms):
    levels, height, width = east.shape
    lane = lanes((height, width))
    depth = count[...]
    packed = [jnp.zeros((height, width), F32) for _ in range(3)]
    for k in range(levels):
        here = (lane >> 1) == k
        for t in range(2):
            x = tracers[t, k]
            packed[t] = jnp.where(here, turn(x, 2 * k + 1), packed[t])
            tops[t, k : k + 1, :] = x[height - 1 :, :]
            bottoms[t, k : k + 1, :] = x[:1, :]
        packed[2] = jnp.where(here, turn(east[k], 2 * k + 1), packed[2])
        tops[2, k : k + 1, :] = north[k, height - 1 :, :]
    for t in range(2):
        first[t] = tracers[t, 0]
        tile[t] = packed[t]
    spare = tops.shape[1] - levels
    for t in range(3):
        tops[t, levels:, :] = jnp.zeros((spare, width), F32)
    for t in range(2):
        bottoms[t, levels:, :] = jnp.zeros((spare, width), F32)
    even = (lane & 1) == 0
    wet_last = jnp.where((lane >> 1) < depth[:, width - 1 :], 1.0, 0.0)
    wet_first = jnp.where((lane >> 1) < depth[:, :1], 1.0, 0.0)
    tile[2] = jnp.where(even, packed[2] * wet_last, wet_first)
    tall = sublanes(tops.shape[1:])
    tops[2] = tops[2] * jnp.where(tall < depth[height - 1 :, :], 1.0, 0.0)
    bottoms[2] = jnp.where(tall < depth[:1, :], 1.0, 0.0)


def solver_kernel(after, east, north, mixing, count, face_e, face_w, face_n, face_s, inv, low, ratio):
    levels, height, width = east.shape
    lane, row = lanes((height, width)), sublanes((height, width))
    depth = count[...]
    depth_e = jnp.where(lane == width - 1, levels, turn(depth, -1))
    depth_n = jnp.where(row == height - 1, levels, pltpu.roll(depth, height - 1, 0))
    depth_e = jnp.minimum(depth, depth_e)
    depth_n = jnp.minimum(depth, depth_n)
    a_prev = r_prev = jnp.zeros((height, width), F32)
    for k in range(levels):
        ce = jnp.where(depth_e > k, east[k], 0.0)
        cn = jnp.where(depth_n > k, north[k], 0.0)
        face_e[k] = ce
        face_w[k] = turn(ce, 1)
        face_n[k] = cn
        face_s[k] = pltpu.roll(cn, 1, 0)
        a = jnp.where(depth > k + 1, mixing[k], 0.0) if k + 1 < levels else jnp.zeros((height, width), F32)
        iv = 1.0 / (1.0 + a_prev + a - a_prev * r_prev)
        inv[k] = iv
        low[k] = a_prev * iv
        r_prev = a * iv
        ratio[k] = r_prev
        a_prev = a


def force_kernel(
    place, index, a0, a1, a2, weights, count, first, tile, tops, bottoms,
    forced, sent, out_r0, out_r1, held, picked,
):
    height, width = count.shape
    blocks = held.shape[1] // 2
    for s, a in enumerate((a0, a1, a2)):
        held[s] = a[: 2 * blocks].astype(F32)
    for y in range(height):
        for s in range(3):
            b = lax.rem(index[y, 0, s], blocks)
            for f in range(2):
                picked[8 * y + f : 8 * y + f + 1, s * 128 : (s + 1) * 128] = held[
                    s, pl.ds(b + f * blocks, 1), :
                ]
    wet = jnp.where(count[...] > 0, 0.5, 0.0)
    for y in range(height):
        got = jnp.dot(
            picked[8 * y : 8 * y + 8].astype(BF16), weights[y], preferred_element_type=F32
        )
        for f in range(2):
            forced[f, y : y + 1, :] = got[f : f + 1, :]
    here = lanes((height, width)) < 2
    even = place[0] == 0
    out_r0[...] = jnp.where(even, tops[...], bottoms[...])
    out_r1[...] = jnp.where(even, bottoms[...], tops[...])
    sent[2] = tile[2]
    for t in range(2):
        x = first[t] + wet * forced[t]
        forced[t] = x
        sent[t] = jnp.where(here, turn(x, 1), tile[t])
        top, bottom = x[height - 1 :, :], x[:1, :]
        out_r0[t, :1, :] = jnp.where(even, top, bottom)
        out_r1[t, :1, :] = jnp.where(even, bottom, top)


def step(place, field, level0, face_e, face_w, face_n, face_s, inv, low, ratio,
         own_c, got_c, own_r, got_r, coef_c, coef_r, solved, edge_n, edge_s, out, messages):
    levels, height, width = face_e.shape
    lane, row = lanes((height, width)), sublanes((height, width))
    even_r, even_c = place[0] == 0, place[1] == 0
    even = (lane & 1) == 0

    def facing(own, pair):
        a, b = pair
        from_e, from_w = jnp.where(even_c, a, b), jnp.where(even_c, b, a)
        theirs = jnp.where(even, from_w, from_e)
        mine = jnp.where(even, turn(own, -1), turn(own, 1))
        return theirs, mine

    c_theirs, c_mine = facing(*coef_c)
    c = c_theirs * c_mine
    edges = []
    for t in range(2):
        theirs, mine = facing(own_c[t], (got_c[0][t], got_c[1][t]))
        flux = c * jnp.where((c > 0) == even, theirs, mine)
        edges.append(jnp.where(even, flux, turn(flux, -2)))

    def row_pair(a, b):
        return jnp.where(even_r, a, b), jnp.where(even_r, b, a)

    own_n, own_s = row_pair(coef_r[0][...], coef_r[1][...])
    from_n, from_s = row_pair(coef_r[2][...], coef_r[3][...])
    cn_row, cs_row = own_n * from_n, own_s * from_s
    for t in range(2):
        own_n, own_s = row_pair(own_r[0][t], own_r[1][t])
        from_n, from_s = row_pair(got_r[0][t], got_r[1][t])
        edge_n[t] = cn_row * jnp.where(cn_row > 0, own_n, from_n)
        edge_s[t] = cs_row * jnp.where(cs_row > 0, from_s, own_s)

    east_end, west_end = lane == width - 1, lane == 0
    north_end, south_end = row == height - 1, row == 0
    value = [None, None]
    for k in range(levels):
        ce, cw, cn, cs = face_e[k], face_w[k], face_n[k], face_s[k]
        for t in range(2):
            x = level0[t] if (k == 0 and level0 is not None) else field[t, k]
            edge = turn(edges[t], -2 * k)
            fe = jnp.where(east_end, edge, ce * jnp.where(ce > 0, x, turn(x, -1)))
            fw = jnp.where(west_end, edge, cw * jnp.where(cw > 0, turn(x, 1), x))
            fn = cn * jnp.where(cn > 0, x, pltpu.roll(x, height - 1, 0))
            fn = jnp.where(north_end, edge_n[t, k : k + 1, :], fn)
            fs = cs * jnp.where(cs > 0, pltpu.roll(x, 1, 0), x)
            fs = jnp.where(south_end, edge_s[t, k : k + 1, :], fs)
            now = (x - (fe - fw) - (fn - fs)) * inv[k]
            if k:
                now = now + low[k] * value[t]
            value[t] = now
            solved[t, k] = now
    packed = [jnp.zeros((height, width), F32)] * 2
    for k in range(levels - 1, -1, -1):
        for t in range(2):
            if k < levels - 1:
                value[t] = solved[t, k] + ratio[k] * value[t]
            y = value[t]
            out[t, k] = y
            if messages is not None:
                packed[t] = jnp.where((lane >> 1) == k, turn(y, 2 * k + 1), packed[t])
                top, bottom = y[height - 1 :, :], y[:1, :]
                messages[1][t, k : k + 1, :] = jnp.where(even_r, top, bottom)
                messages[2][t, k : k + 1, :] = jnp.where(even_r, bottom, top)
    if messages is not None:
        spare = messages[1].shape[1] - levels
        for t in range(2):
            messages[0][t] = packed[t]
            messages[1][t, levels:, :] = jnp.zeros((spare, width), F32)
            messages[2][t, levels:, :] = jnp.zeros((spare, width), F32)


def first_step_kernel(
    place, tracers, forced, face_e, face_w, face_n, face_s, inv, low, ratio,
    c, c0, c1, r0, r1, g0, g1, out, out_c, out_r0, out_r1, solved, edge_n, edge_s,
):
    step(place, tracers, forced, face_e, face_w, face_n, face_s, inv, low, ratio,
         c, (c0, c1), (r0, r1), (g0, g1), (c[2], (c0[2], c1[2])),
         (r0.at[2], r1.at[2], g0.at[2], g1.at[2]), solved, edge_n, edge_s, out, (out_c, out_r0, out_r1))


def second_step_kernel(
    place, field, face_e, face_w, face_n, face_s, inv, low, ratio,
    c, c0, c1, r0, r1, g0, g1, d, d0, d1, u0, u1, h0, h1, out, solved, edge_n, edge_s,
):
    step(place, field, None, face_e, face_w, face_n, face_s, inv, low, ratio,
         d, (d0, d1), (u0, u1), (h0, h1), (c[2], (c0[2], c1[2])),
         (r0.at[2], r1.at[2], g0.at[2], g1.at[2]), solved, edge_n, edge_s, out, None)


def gather_kernel(after, wanted, atm, out0, out1, out2):
    for s, out in enumerate((out0, out1, out2)):
        for y in range(out.shape[0]):
            out[y] = atm[wanted[s * out.shape[0] + y]]


def remap_kernel(a0, a1, a2, weights, out):
    for y in range(out.shape[1]):
        picked = jnp.concatenate([a0[y], a1[y], a2[y]], 1)
        out[:, y, :] = jnp.dot(picked, weights[y], preferred_element_type=F32)


def call(kernel, outs, specs, scratch=(), cost=1, limit=LIMIT):
    return pl.pallas_call(
        kernel,
        out_shape=outs,
        in_specs=specs,
        out_specs=[VMEM] * len(outs),
        scratch_shapes=list(scratch),
        compiler_params=pltpu.CompilerParams(vmem_limit_bytes=limit),
        cost_estimate=pl.CostEstimate(flops=0, bytes_accessed=cost * 3000000, transcendentals=0),
    )


def swap(block, axis, pairs):
    return lax.ppermute(block, axis, [(a, b) for a, b in pairs] + [(b, a) for a, b in pairs])


def per_device(
    atm_flux, remap_weights, intersection, tracers, east_speed, north_speed, mixing, level_count
):
    tiles, groups = lax.axis_size("cols"), lax.axis_size("rows")
    levels, height, width = east_speed.shape
    tall = -(-levels // 8) * 8
    sds = lambda *shape, dtype=F32: jax.ShapeDtypeStruct(shape, dtype)

    def from_ahead(block, distance):
        return lax.ppermute(block, "cols", [((i + distance) % tiles, i) for i in range(tiles)])

    cols0 = [(i, i + 1) for i in range(0, tiles, 2)]
    cols1 = [(i, (i + 1) % tiles) for i in range(1, tiles, 2)]
    rows0 = [(i, i + 1) for i in range(0, groups - 1, 2)]
    rows1 = [(i, i + 1) for i in range(1, groups - 1, 2)]

    place = jnp.stack([lax.axis_index("rows") % 2, lax.axis_index("cols") % 2]).astype(jnp.int32)
    weights = remap_weights.reshape(height, -1, width)

    blocks, fields = atm_flux.shape[:2]
    (few,) = call(
        ask_kernel,
        [sds(2 * blocks + 3 * height, width, dtype=BF16)],
        [SMEM, ANY],
        [
            pltpu.VMEM((blocks, 16, width), BF16),
            pltpu.VMEM((2 * blocks + 3 * height, width), F32),
            pltpu.SemaphoreType.DMA,
        ],
        cost=1,
        limit=FULL,
    )(intersection, atm_flux)
    slots = [tiles // 2 + s - 1 for s in range(3)]
    part = [from_ahead(few, d) for d in slots]

    plane = sds(levels, height, width)
    first, tile, tops, bottoms = call(
        pack_kernel,
        [sds(2, height, width), sds(3, height, width)] + [sds(3, tall, width)] * 2,
        [VMEM] * 4,
        cost=2,
    )(tracers, east_speed, north_speed, level_count)

    forced, c, r0, r1 = call(
        force_kernel,
        [sds(2, height, width), sds(3, height, width)] + [sds(3, tall, width)] * 2,
        [SMEM, SMEM] + [VMEM] * 9,
        [pltpu.VMEM((3, 2 * blocks, width), F32), pltpu.VMEM((8 * height, 3 * width), F32)],
        cost=1,
    )(place, intersection, *part, weights, level_count, first, tile, tops, bottoms)

    def exchange(c, r0, r1):
        g0, g1 = swap(r0, "rows", rows0), swap(r1, "rows", rows1)
        return swap(c, "cols", cols0), swap(c, "cols", cols1), g0, g1

    c0, c1, g0, g1 = exchange(c, r0, r1)
    coefficients = call(solver_kernel, [plane] * 7, [ANY] + [VMEM] * 4, cost=4)(
        c, east_speed, north_speed, mixing, level_count
    )
    wanted = jnp.concatenate(
        [part[s][2 * blocks + (2 - s) * height :][:height, 0] for s in range(3)]
    ).astype(jnp.int32)
    found = call(
        gather_kernel,
        [sds(height, fields, width, dtype=BF16)] * 3,
        [ANY, SMEM, VMEM],
        cost=1,
    )(c, wanted, atm_flux)
    blocks_of = [from_ahead(found[2 - s], slots[s]) for s in range(3)]

    scratch = [pltpu.VMEM((2, levels, height, width), F32)] + [pltpu.VMEM((2, tall, width), F32)] * 2
    field, d, u0, u1 = call(
        first_step_kernel,
        [sds(2, levels, height, width), sds(2, height, width)] + [sds(2, tall, width)] * 2,
        [SMEM] + [VMEM] * 16,
        scratch,
        cost=4,
    )(place, tracers, forced, *coefficients, c, c0, c1, r0, r1, g0, g1)
    d0, d1, h0, h1 = exchange(d, u0, u1)
    (ocean_flux,) = call(remap_kernel, [sds(fields, height, width)], [VMEM] * 4, cost=2)(
        *blocks_of, weights
    )
    (result,) = call(
        second_step_kernel,
        [sds(2, levels, height, width)],
        [SMEM] + [VMEM] * 22,
        scratch,
        cost=3,
    )(place, field, *coefficients, c, c0, c1, r0, r1, g0, g1, d, d0, d1, u0, u1, h0, h1)
    return (ocean_flux, result)


def solution(mesh):
    placed = (
        P(("rows", "cols"), None, None),
        P("rows", None, None, "cols"),
        P("rows", "cols", None),
        P(None, None, "rows", "cols"),
        P(None, "rows", "cols"),
        P(None, "rows", "cols"),
        P(None, "rows", "cols"),
        P("rows", "cols"),
    )
    return jax.shard_map(
        per_device,
        mesh=mesh,
        in_specs=placed,
        out_specs=(P(None, "rows", "cols"), P(None, None, "rows", "cols")),
        check_vma=False,
    )
```

```python
import jax
import jax.numpy as jnp
from jax import lax
from jax.experimental import pallas as pl
from jax.experimental.pallas import tpu as pltpu
from jax.sharding import PartitionSpec as P

F32 = jnp.float32
BF16 = jnp.bfloat16
VMEM = pl.BlockSpec(memory_space=pltpu.VMEM)
ANY = pl.BlockSpec(memory_space=pl.ANY)
SMEM = pl.BlockSpec(memory_space=pltpu.SMEM)
LIMIT = 24 * 1024 * 1024
FULL = 60 * 1024 * 1024


def lanes(shape):
    return lax.broadcasted_iota(jnp.int32, shape, len(shape) - 1)


def sublanes(shape):
    return lax.broadcasted_iota(jnp.int32, shape, len(shape) - 2)


def turn(x, shift):
    shift = shift % x.shape[-1]
    return x if shift == 0 else pltpu.roll(x, shift, x.ndim - 1)


def ask_kernel(index_hbm, atm, out, held, wide, index, sems):
    blocks, rows = held.shape[:2]
    parts = sems.shape[0] - 1
    fetch = pltpu.make_async_copy(index_hbm, index, sems.at[parts])
    fetch.start()
    share = blocks // parts
    copies = [
        pltpu.make_async_copy(
            atm.at[p * share : (p + 1) * share, :rows, :], held.at[p * share : (p + 1) * share], sems.at[p]
        )
        for p in range(parts)
    ]
    for copy in copies:
        copy.start()
    height = index.shape[2]
    fetch.wait()
    for s in range(3):
        for y in range(height):
            at = 2 * blocks + s * height + y
            b = lax.rem(index[s, 0, y], blocks).astype(F32)
            wide[at : at + 1, :] = jnp.full((1, wide.shape[1]), b, F32)
    for p in range(parts):
        copies[p].wait()
        for b in range(p * share, (p + 1) * share):
            x = held[b].astype(F32)
            for f in range(2):
                wide[b + f * blocks : b + f * blocks + 1, :] = x[f : f + 1, :]
    out[...] = wide[...].astype(BF16)


def pack_kernel(tracers, east, north, count, first, tile, tops, bottoms):
    levels, height, width = east.shape
    lane = lanes((height, width))
    depth = count[...]
    packed = [jnp.zeros((height, width), F32) for _ in range(3)]
    for k in range(levels):
        here = (lane >> 1) == k
        for t in range(2):
            x = tracers[t, k]
            packed[t] = jnp.where(here, turn(x, 2 * k + 1), packed[t])
            tops[t, k : k + 1, :] = x[height - 1 :, :]
            bottoms[t, k : k + 1, :] = x[:1, :]
        packed[2] = jnp.where(here, turn(east[k], 2 * k + 1), packed[2])
        tops[2, k : k + 1, :] = north[k, height - 1 :, :]
    for t in range(2):
        first[t] = tracers[t, 0]
        tile[t] = packed[t]
    spare = tops.shape[1] - levels
    for t in range(3):
        tops[t, levels:, :] = jnp.zeros((spare, width), F32)
    for t in range(2):
        bottoms[t, levels:, :] = jnp.zeros((spare, width), F32)
    even = (lane & 1) == 0
    wet_last = jnp.where((lane >> 1) < depth[:, width - 1 :], 1.0, 0.0)
    wet_first = jnp.where((lane >> 1) < depth[:, :1], 1.0, 0.0)
    tile[2] = jnp.where(even, packed[2] * wet_last, wet_first)
    tall = sublanes(tops.shape[1:])
    tops[2] = tops[2] * jnp.where(tall < depth[height - 1 :, :], 1.0, 0.0)
    bottoms[2] = jnp.where(tall < depth[:1, :], 1.0, 0.0)


def solver_kernel(after, east, north, mixing, count, face_e, face_w, face_n, face_s, inv, low, ratio):
    levels, height, width = east.shape
    lane, row = lanes((height, width)), sublanes((height, width))
    depth = count[...]
    depth_e = jnp.where(lane == width - 1, levels, turn(depth, -1))
    depth_n = jnp.where(row == height - 1, levels, pltpu.roll(depth, height - 1, 0))
    depth_e = jnp.minimum(depth, depth_e)
    depth_n = jnp.minimum(depth, depth_n)
    a_prev = r_prev = jnp.zeros((height, width), F32)
    for k in range(levels):
        ce = jnp.where(depth_e > k, east[k], 0.0)
        cn = jnp.where(depth_n > k, north[k], 0.0)
        face_e[k] = ce
        face_w[k] = turn(ce, 1)
        face_n[k] = cn
        face_s[k] = pltpu.roll(cn, 1, 0)
        a = jnp.where(depth > k + 1, mixing[k], 0.0) if k + 1 < levels else jnp.zeros((height, width), F32)
        iv = 1.0 / (1.0 + a_prev + a - a_prev * r_prev)
        inv[k] = iv
        low[k] = a_prev * iv
        r_prev = a * iv
        ratio[k] = r_prev
        a_prev = a


def force_kernel(
    place, index, a0, a1, a2, weights, count, first, tile, tops, bottoms,
    forced, sent, out_r0, out_r1, held, picked,
):
    height, width = count.shape
    blocks = held.shape[1] // 2
    for s, a in enumerate((a0, a1, a2)):
        held[s] = a[: 2 * blocks].astype(F32)
    for y in range(height):
        for s in range(3):
            b = lax.rem(index[s, 0, y], blocks)
            for f in range(2):
                picked[8 * y + f : 8 * y + f + 1, s * 128 : (s + 1) * 128] = held[
                    s, pl.ds(b + f * blocks, 1), :
                ]
    wet = jnp.where(count[...] > 0, 0.5, 0.0)
    for y in range(height):
        got = jnp.dot(
            picked[8 * y : 8 * y + 8].astype(BF16), weights[y], preferred_element_type=F32
        )
        for f in range(2):
            forced[f, y : y + 1, :] = got[f : f + 1, :]
    here = lanes((height, width)) < 2
    even = place[0] == 0
    out_r0[...] = jnp.where(even, tops[...], bottoms[...])
    out_r1[...] = jnp.where(even, bottoms[...], tops[...])
    sent[2] = tile[2]
    for t in range(2):
        x = first[t] + wet * forced[t]
        forced[t] = x
        sent[t] = jnp.where(here, turn(x, 1), tile[t])
        top, bottom = x[height - 1 :, :], x[:1, :]
        out_r0[t, :1, :] = jnp.where(even, top, bottom)
        out_r1[t, :1, :] = jnp.where(even, bottom, top)


def step(place, field, level0, face_e, face_w, face_n, face_s, inv, low, ratio,
         own_c, got_c, own_r, got_r, coef_c, coef_r, solved, edge_n, edge_s, out, messages):
    levels, height, width = face_e.shape
    lane, row = lanes((height, width)), sublanes((height, width))
    even_r, even_c = place[0] == 0, place[1] == 0
    even = (lane & 1) == 0

    def facing(own, pair):
        a, b = pair
        from_e, from_w = jnp.where(even_c, a, b), jnp.where(even_c, b, a)
        theirs = jnp.where(even, from_w, from_e)
        mine = jnp.where(even, turn(own, -1), turn(own, 1))
        return theirs, mine

    c_theirs, c_mine = facing(*coef_c)
    c = c_theirs * c_mine
    edges = []
    for t in range(2):
        theirs, mine = facing(own_c[t], (got_c[0][t], got_c[1][t]))
        flux = c * jnp.where((c > 0) == even, theirs, mine)
        edges.append(jnp.where(even, flux, turn(flux, -2)))

    def row_pair(a, b):
        return jnp.where(even_r, a, b), jnp.where(even_r, b, a)

    own_n, own_s = row_pair(coef_r[0][...], coef_r[1][...])
    from_n, from_s = row_pair(coef_r[2][...], coef_r[3][...])
    cn_row, cs_row = own_n * from_n, own_s * from_s
    for t in range(2):
        own_n, own_s = row_pair(own_r[0][t], own_r[1][t])
        from_n, from_s = row_pair(got_r[0][t], got_r[1][t])
        edge_n[t] = cn_row * jnp.where(cn_row > 0, own_n, from_n)
        edge_s[t] = cs_row * jnp.where(cs_row > 0, from_s, own_s)

    east_end, west_end = lane == width - 1, lane == 0
    north_end, south_end = row == height - 1, row == 0
    value = [None, None]
    for k in range(levels):
        ce, cw, cn, cs = face_e[k], face_w[k], face_n[k], face_s[k]
        for t in range(2):
            x = level0[t] if (k == 0 and level0 is not None) else field[t, k]
            edge = turn(edges[t], -2 * k)
            fe = jnp.where(east_end, edge, ce * jnp.where(ce > 0, x, turn(x, -1)))
            fw = jnp.where(west_end, edge, cw * jnp.where(cw > 0, turn(x, 1), x))
            fn = cn * jnp.where(cn > 0, x, pltpu.roll(x, height - 1, 0))
            fn = jnp.where(north_end, edge_n[t, k : k + 1, :], fn)
            fs = cs * jnp.where(cs > 0, pltpu.roll(x, 1, 0), x)
            fs = jnp.where(south_end, edge_s[t, k : k + 1, :], fs)
            now = (x - (fe - fw) - (fn - fs)) * inv[k]
            if k:
                now = now + low[k] * value[t]
            value[t] = now
            solved[t, k] = now
    packed = [jnp.zeros((height, width), F32)] * 2
    for k in range(levels - 1, -1, -1):
        for t in range(2):
            if k < levels - 1:
                value[t] = solved[t, k] + ratio[k] * value[t]
            y = value[t]
            out[t, k] = y
            if messages is not None:
                packed[t] = jnp.where((lane >> 1) == k, turn(y, 2 * k + 1), packed[t])
                top, bottom = y[height - 1 :, :], y[:1, :]
                messages[1][t, k : k + 1, :] = jnp.where(even_r, top, bottom)
                messages[2][t, k : k + 1, :] = jnp.where(even_r, bottom, top)
    if messages is not None:
        spare = messages[1].shape[1] - levels
        for t in range(2):
            messages[0][t] = packed[t]
            messages[1][t, levels:, :] = jnp.zeros((spare, width), F32)
            messages[2][t, levels:, :] = jnp.zeros((spare, width), F32)


def first_step_kernel(
    place, tracers, forced, face_e, face_w, face_n, face_s, inv, low, ratio,
    c, c0, c1, r0, r1, g0, g1, out, out_c, out_r0, out_r1, solved, edge_n, edge_s,
):
    step(place, tracers, forced, face_e, face_w, face_n, face_s, inv, low, ratio,
         c, (c0, c1), (r0, r1), (g0, g1), (c[2], (c0[2], c1[2])),
         (r0.at[2], r1.at[2], g0.at[2], g1.at[2]), solved, edge_n, edge_s, out, (out_c, out_r0, out_r1))


def second_step_kernel(
    place, field, face_e, face_w, face_n, face_s, inv, low, ratio,
    c, c0, c1, r0, r1, g0, g1, d, d0, d1, u0, u1, h0, h1, out, solved, edge_n, edge_s,
):
    step(place, field, None, face_e, face_w, face_n, face_s, inv, low, ratio,
         d, (d0, d1), (u0, u1), (h0, h1), (c[2], (c0[2], c1[2])),
         (r0.at[2], r1.at[2], g0.at[2], g1.at[2]), solved, edge_n, edge_s, out, None)


def gather_kernel(after, wanted, atm, *outs):
    for s, out in enumerate(outs):
        for y in range(out.shape[0]):
            out[y] = atm[wanted[s * out.shape[0] + y]]


def remap_kernel(a0, a1, a2, weights, out):
    for y in range(out.shape[1]):
        picked = jnp.concatenate([a0[y], a1[y], a2[y]], 1)
        out[:, y, :] = jnp.dot(picked, weights[y], preferred_element_type=F32)


def call(kernel, outs, specs, scratch=(), cost=1, limit=LIMIT):
    return pl.pallas_call(
        kernel,
        out_shape=outs,
        in_specs=specs,
        out_specs=[VMEM] * len(outs),
        scratch_shapes=list(scratch),
        compiler_params=pltpu.CompilerParams(vmem_limit_bytes=limit),
        cost_estimate=pl.CostEstimate(flops=cost * 2000000000, bytes_accessed=cost * 3000000, transcendentals=0),
    )


def swap(block, axis, pairs):
    return lax.ppermute(block, axis, [(a, b) for a, b in pairs] + [(b, a) for a, b in pairs])


def per_device(
    atm_flux, remap_weights, intersection, tracers, east_speed, north_speed, mixing, level_count
):
    tiles, groups = lax.axis_size("cols"), lax.axis_size("rows")
    levels, height, width = east_speed.shape
    tall = -(-levels // 8) * 8
    sds = lambda *shape, dtype=F32: jax.ShapeDtypeStruct(shape, dtype)

    def from_ahead(block, distance):
        return lax.ppermute(block, "cols", [((i + distance) % tiles, i) for i in range(tiles)])

    cols0 = [(i, i + 1) for i in range(0, tiles, 2)]
    cols1 = [(i, (i + 1) % tiles) for i in range(1, tiles, 2)]
    rows0 = [(i, i + 1) for i in range(0, groups - 1, 2)]
    rows1 = [(i, i + 1) for i in range(1, groups - 1, 2)]

    place = jnp.stack([lax.axis_index("rows") % 2, lax.axis_index("cols") % 2]).astype(jnp.int32)
    weights = remap_weights.reshape(height, -1, width)

    blocks, fields = atm_flux.shape[:2]
    index = intersection.transpose(2, 1, 0)
    (few,) = call(
        ask_kernel,
        [sds(2 * blocks + 3 * height, width, dtype=BF16)],
        [ANY, ANY],
        [
            pltpu.VMEM((blocks, 16, width), BF16),
            pltpu.VMEM((2 * blocks + 3 * height, width), F32),
            pltpu.SMEM((3, 1, height), jnp.int32),
            pltpu.SemaphoreType.DMA((5,)),
        ],
        cost=1,
        limit=FULL,
    )(index, atm_flux)
    slots = [tiles // 2 + s - 1 for s in range(3)]
    part = [from_ahead(few, d) for d in slots]

    plane = sds(levels, height, width)
    first, tile, tops, bottoms = call(
        pack_kernel,
        [sds(2, height, width), sds(3, height, width)] + [sds(3, tall, width)] * 2,
        [VMEM] * 4,
        cost=2,
    )(tracers, east_speed, north_speed, level_count)

    forced, c, r0, r1 = call(
        force_kernel,
        [sds(2, height, width), sds(3, height, width)] + [sds(3, tall, width)] * 2,
        [SMEM, SMEM] + [VMEM] * 9,
        [pltpu.VMEM((3, 2 * blocks, width), F32), pltpu.VMEM((8 * height, 3 * width), F32)],
        cost=1,
    )(place, index, *part, weights, level_count, first, tile, tops, bottoms)

    def exchange(c, r0, r1):
        g0, g1 = swap(r0, "rows", rows0), swap(r1, "rows", rows1)
        return swap(c, "cols", cols0), swap(c, "cols", cols1), g0, g1

    c0, c1, g0, g1 = exchange(c, r0, r1)
    coefficients = call(solver_kernel, [plane] * 7, [ANY] + [VMEM] * 4, cost=4)(
        c, east_speed, north_speed, mixing, level_count
    )
    def wanted(*which):
        return jnp.concatenate(
            [part[s][2 * blocks + (2 - s) * height :][:height, 0] for s in which]
        ).astype(jnp.int32)

    def answers(after, *which):
        found = call(
            gather_kernel,
            [sds(height, fields, width, dtype=BF16)] * len(which),
            [ANY, SMEM, VMEM],
            cost=1,
        )(after, wanted(*which), atm_flux)
        return [from_ahead(block, slots[2 - s]) for s, block in zip(which, found)]

    blocks2, blocks1, blocks0 = answers(c, 0, 1, 2)
    scratch = [pltpu.VMEM((2, levels, height, width), F32)] + [pltpu.VMEM((2, tall, width), F32)] * 2
    field, d, u0, u1 = call(
        first_step_kernel,
        [sds(2, levels, height, width), sds(2, height, width)] + [sds(2, tall, width)] * 2,
        [SMEM] + [VMEM] * 16,
        scratch,
        cost=4,
    )(place, tracers, forced, *coefficients, c, c0, c1, r0, r1, g0, g1)
    d0, d1, h0, h1 = exchange(d, u0, u1)
    (ocean_flux,) = call(remap_kernel, [sds(fields, height, width)], [VMEM] * 4, cost=2)(
        blocks0, blocks1, blocks2, weights
    )
    (result,) = call(
        second_step_kernel,
        [sds(2, levels, height, width)],
        [SMEM] + [VMEM] * 22,
        scratch,
        cost=3,
    )(place, field, *coefficients, c, c0, c1, r0, r1, g0, g1, d, d0, d1, u0, u1, h0, h1)
    return (ocean_flux, result)


def solution(mesh):
    placed = (
        P(("rows", "cols"), None, None),
        P("rows", None, None, "cols"),
        P("rows", "cols", None),
        P(None, None, "rows", "cols"),
        P(None, "rows", "cols"),
        P(None, "rows", "cols"),
        P(None, "rows", "cols"),
        P("rows", "cols"),
    )
    return jax.shard_map(
        per_device,
        mesh=mesh,
        in_specs=placed,
        out_specs=(P(None, "rows", "cols"), P(None, None, "rows", "cols")),
        check_vma=False,
    )
```

```python
import jax
import jax.numpy as jnp
from jax import lax
from jax.experimental import pallas as pl
from jax.experimental.pallas import tpu as pltpu
from jax.sharding import PartitionSpec as P

F32 = jnp.float32
BF16 = jnp.bfloat16
VMEM = pl.BlockSpec(memory_space=pltpu.VMEM)
ANY = pl.BlockSpec(memory_space=pl.ANY)
SMEM = pl.BlockSpec(memory_space=pltpu.SMEM)
LIMIT = 24 * 1024 * 1024
FULL = 60 * 1024 * 1024


def lanes(shape):
    return lax.broadcasted_iota(jnp.int32, shape, len(shape) - 1)


def sublanes(shape):
    return lax.broadcasted_iota(jnp.int32, shape, len(shape) - 2)


def turn(x, shift):
    shift = shift % x.shape[-1]
    return x if shift == 0 else pltpu.roll(x, shift, x.ndim - 1)


def ask_kernel(index_hbm, atm, out, held, wide, index, sems):
    blocks, rows = held.shape[:2]
    parts = sems.shape[0] - 1
    fetch = pltpu.make_async_copy(index_hbm, index, sems.at[parts])
    fetch.start()
    share = blocks // parts
    copies = [
        pltpu.make_async_copy(
            atm.at[p * share : (p + 1) * share, :rows, :], held.at[p * share : (p + 1) * share], sems.at[p]
        )
        for p in range(parts)
    ]
    for copy in copies:
        copy.start()
    height = index.shape[2]
    fetch.wait()
    for s in range(3):
        for y in range(height):
            at = 2 * blocks + s * height + y
            b = lax.rem(index[s, 0, y], blocks).astype(F32)
            wide[at : at + 1, :] = jnp.full((1, wide.shape[1]), b, F32)
    for p in range(parts):
        copies[p].wait()
        for b in range(p * share, (p + 1) * share):
            x = held[b].astype(F32)
            for f in range(2):
                wide[b + f * blocks : b + f * blocks + 1, :] = x[f : f + 1, :]
    out[...] = wide[...].astype(BF16)


def pack_kernel(tracers, east, north, count, first, tile, tops, bottoms):
    levels, height, width = east.shape
    lane = lanes((height, width))
    depth = count[...]
    packed = [jnp.zeros((height, width), F32) for _ in range(3)]
    for k in range(levels):
        here = (lane >> 1) == k
        for t in range(2):
            x = tracers[t, k]
            packed[t] = jnp.where(here, turn(x, 2 * k + 1), packed[t])
            tops[t, k : k + 1, :] = x[height - 1 :, :]
            bottoms[t, k : k + 1, :] = x[:1, :]
        packed[2] = jnp.where(here, turn(east[k], 2 * k + 1), packed[2])
        tops[2, k : k + 1, :] = north[k, height - 1 :, :]
    for t in range(2):
        first[t] = tracers[t, 0]
        tile[t] = packed[t]
    spare = tops.shape[1] - levels
    for t in range(3):
        tops[t, levels:, :] = jnp.zeros((spare, width), F32)
    for t in range(2):
        bottoms[t, levels:, :] = jnp.zeros((spare, width), F32)
    even = (lane & 1) == 0
    wet_last = jnp.where((lane >> 1) < depth[:, width - 1 :], 1.0, 0.0)
    wet_first = jnp.where((lane >> 1) < depth[:, :1], 1.0, 0.0)
    tile[2] = jnp.where(even, packed[2] * wet_last, wet_first)
    tall = sublanes(tops.shape[1:])
    tops[2] = tops[2] * jnp.where(tall < depth[height - 1 :, :], 1.0, 0.0)
    bottoms[2] = jnp.where(tall < depth[:1, :], 1.0, 0.0)


def solver_kernel(after, east, north, mixing, count, face_e, face_w, face_n, face_s, inv, low, ratio):
    levels, height, width = east.shape
    lane, row = lanes((height, width)), sublanes((height, width))
    depth = count[...]
    depth_e = jnp.where(lane == width - 1, levels, turn(depth, -1))
    depth_n = jnp.where(row == height - 1, levels, pltpu.roll(depth, height - 1, 0))
    depth_e = jnp.minimum(depth, depth_e)
    depth_n = jnp.minimum(depth, depth_n)
    a_prev = r_prev = jnp.zeros((height, width), F32)
    for k in range(levels):
        ce = jnp.where(depth_e > k, east[k], 0.0)
        cn = jnp.where(depth_n > k, north[k], 0.0)
        face_e[k] = ce
        face_w[k] = turn(ce, 1)
        face_n[k] = cn
        face_s[k] = pltpu.roll(cn, 1, 0)
        a = jnp.where(depth > k + 1, mixing[k], 0.0) if k + 1 < levels else jnp.zeros((height, width), F32)
        iv = 1.0 / (1.0 + a_prev + a - a_prev * r_prev)
        inv[k] = iv
        low[k] = a_prev * iv
        r_prev = a * iv
        ratio[k] = r_prev
        a_prev = a


def force_kernel(
    place, index, a0, a1, a2, weights, count, first, tile, tops, bottoms,
    forced, sent, out_r0, out_r1, wanted, held, picked,
):
    height, width = count.shape
    blocks = held.shape[1] // 2
    for s, a in enumerate((a0, a1, a2)):
        held[s] = a[: 2 * blocks].astype(F32)
        start = 2 * blocks + (2 - s) * height
        asked = a[start : start + height].astype(F32)
        own = lanes((height, width)) == sublanes((height, width))
        wanted[s : s + 1, :] = jnp.sum(jnp.where(own, asked, 0.0), 0, keepdims=True).astype(jnp.int32)
    for y in range(height):
        for s in range(3):
            b = lax.rem(index[s, 0, y], blocks)
            for f in range(2):
                picked[8 * y + f : 8 * y + f + 1, s * 128 : (s + 1) * 128] = held[
                    s, pl.ds(b + f * blocks, 1), :
                ]
    wet = jnp.where(count[...] > 0, 0.5, 0.0)
    for y in range(height):
        got = jnp.dot(
            picked[8 * y : 8 * y + 8].astype(BF16), weights[y], preferred_element_type=F32
        )
        for f in range(2):
            forced[f, y : y + 1, :] = got[f : f + 1, :]
    here = lanes((height, width)) < 2
    even = place[0] == 0
    out_r0[...] = jnp.where(even, tops[...], bottoms[...])
    out_r1[...] = jnp.where(even, bottoms[...], tops[...])
    sent[2] = tile[2]
    for t in range(2):
        x = first[t] + wet * forced[t]
        forced[t] = x
        sent[t] = jnp.where(here, turn(x, 1), tile[t])
        top, bottom = x[height - 1 :, :], x[:1, :]
        out_r0[t, :1, :] = jnp.where(even, top, bottom)
        out_r1[t, :1, :] = jnp.where(even, bottom, top)


def step(place, field, level0, face_e, face_w, face_n, face_s, inv, low, ratio,
         own_c, got_c, own_r, got_r, coef_c, coef_r, solved, edge_n, edge_s, out, messages):
    levels, height, width = face_e.shape
    lane, row = lanes((height, width)), sublanes((height, width))
    even_r, even_c = place[0] == 0, place[1] == 0
    even = (lane & 1) == 0

    def facing(own, pair):
        a, b = pair
        from_e, from_w = jnp.where(even_c, a, b), jnp.where(even_c, b, a)
        theirs = jnp.where(even, from_w, from_e)
        mine = jnp.where(even, turn(own, -1), turn(own, 1))
        return theirs, mine

    c_theirs, c_mine = facing(*coef_c)
    c = c_theirs * c_mine
    edges = []
    for t in range(2):
        theirs, mine = facing(own_c[t], (got_c[0][t], got_c[1][t]))
        flux = c * jnp.where((c > 0) == even, theirs, mine)
        edges.append(jnp.where(even, flux, turn(flux, -2)))

    def row_pair(a, b):
        return jnp.where(even_r, a, b), jnp.where(even_r, b, a)

    own_n, own_s = row_pair(coef_r[0][...], coef_r[1][...])
    from_n, from_s = row_pair(coef_r[2][...], coef_r[3][...])
    cn_row, cs_row = own_n * from_n, own_s * from_s
    for t in range(2):
        own_n, own_s = row_pair(own_r[0][t], own_r[1][t])
        from_n, from_s = row_pair(got_r[0][t], got_r[1][t])
        edge_n[t] = cn_row * jnp.where(cn_row > 0, own_n, from_n)
        edge_s[t] = cs_row * jnp.where(cs_row > 0, from_s, own_s)

    east_end, west_end = lane == width - 1, lane == 0
    north_end, south_end = row == height - 1, row == 0
    value = [None, None]
    for k in range(levels):
        ce, cw, cn, cs = face_e[k], face_w[k], face_n[k], face_s[k]
        for t in range(2):
            x = level0[t] if (k == 0 and level0 is not None) else field[t, k]
            edge = turn(edges[t], -2 * k)
            fe = jnp.where(east_end, edge, ce * jnp.where(ce > 0, x, turn(x, -1)))
            fw = jnp.where(west_end, edge, cw * jnp.where(cw > 0, turn(x, 1), x))
            fn = cn * jnp.where(cn > 0, x, pltpu.roll(x, height - 1, 0))
            fn = jnp.where(north_end, edge_n[t, k : k + 1, :], fn)
            fs = cs * jnp.where(cs > 0, pltpu.roll(x, 1, 0), x)
            fs = jnp.where(south_end, edge_s[t, k : k + 1, :], fs)
            now = (x - (fe - fw) - (fn - fs)) * inv[k]
            if k:
                now = now + low[k] * value[t]
            value[t] = now
            solved[t, k] = now
    packed = [jnp.zeros((height, width), F32)] * 2
    for k in range(levels - 1, -1, -1):
        for t in range(2):
            if k < levels - 1:
                value[t] = solved[t, k] + ratio[k] * value[t]
            y = value[t]
            out[t, k] = y
            if messages is not None:
                packed[t] = jnp.where((lane >> 1) == k, turn(y, 2 * k + 1), packed[t])
                top, bottom = y[height - 1 :, :], y[:1, :]
                messages[1][t, k : k + 1, :] = jnp.where(even_r, top, bottom)
                messages[2][t, k : k + 1, :] = jnp.where(even_r, bottom, top)
    if messages is not None:
        spare = messages[1].shape[1] - levels
        for t in range(2):
            messages[0][t] = packed[t]
            messages[1][t, levels:, :] = jnp.zeros((spare, width), F32)
            messages[2][t, levels:, :] = jnp.zeros((spare, width), F32)


def first_step_kernel(
    place, tracers, forced, face_e, face_w, face_n, face_s, inv, low, ratio,
    c, c0, c1, r0, r1, g0, g1, out, out_c, out_r0, out_r1, solved, edge_n, edge_s,
):
    step(place, tracers, forced, face_e, face_w, face_n, face_s, inv, low, ratio,
         c, (c0, c1), (r0, r1), (g0, g1), (c[2], (c0[2], c1[2])),
         (r0.at[2], r1.at[2], g0.at[2], g1.at[2]), solved, edge_n, edge_s, out, (out_c, out_r0, out_r1))


def second_step_kernel(
    place, field, face_e, face_w, face_n, face_s, inv, low, ratio,
    c, c0, c1, r0, r1, g0, g1, d, d0, d1, u0, u1, h0, h1, out, solved, edge_n, edge_s,
):
    step(place, field, None, face_e, face_w, face_n, face_s, inv, low, ratio,
         d, (d0, d1), (u0, u1), (h0, h1), (c[2], (c0[2], c1[2])),
         (r0.at[2], r1.at[2], g0.at[2], g1.at[2]), solved, edge_n, edge_s, out, None)


def gather_kernel(wanted, atm, *outs):
    for s, out in enumerate(outs):
        for y in range(out.shape[0]):
            out[y] = atm[wanted[s, y]]


def remap_kernel(a0, a1, a2, weights, out):
    for y in range(out.shape[1]):
        picked = jnp.concatenate([a0[y], a1[y], a2[y]], 1)
        out[:, y, :] = jnp.dot(picked, weights[y], preferred_element_type=F32)


def call(kernel, outs, specs, scratch=(), cost=1, limit=LIMIT):
    return pl.pallas_call(
        kernel,
        out_shape=outs,
        in_specs=specs,
        out_specs=[VMEM] * len(outs),
        scratch_shapes=list(scratch),
        compiler_params=pltpu.CompilerParams(vmem_limit_bytes=limit),
        cost_estimate=pl.CostEstimate(flops=cost * 2000000000, bytes_accessed=cost * 3000000, transcendentals=0),
    )


def swap(block, axis, pairs):
    return lax.ppermute(block, axis, [(a, b) for a, b in pairs] + [(b, a) for a, b in pairs])


def per_device(
    atm_flux, remap_weights, intersection, tracers, east_speed, north_speed, mixing, level_count
):
    tiles, groups = lax.axis_size("cols"), lax.axis_size("rows")
    levels, height, width = east_speed.shape
    tall = -(-levels // 8) * 8
    sds = lambda *shape, dtype=F32: jax.ShapeDtypeStruct(shape, dtype)

    def from_ahead(block, distance):
        return lax.ppermute(block, "cols", [((i + distance) % tiles, i) for i in range(tiles)])

    cols0 = [(i, i + 1) for i in range(0, tiles, 2)]
    cols1 = [(i, (i + 1) % tiles) for i in range(1, tiles, 2)]
    rows0 = [(i, i + 1) for i in range(0, groups - 1, 2)]
    rows1 = [(i, i + 1) for i in range(1, groups - 1, 2)]

    place = jnp.stack([lax.axis_index("rows") % 2, lax.axis_index("cols") % 2]).astype(jnp.int32)
    weights = remap_weights.reshape(height, -1, width)

    blocks, fields = atm_flux.shape[:2]
    index = intersection.transpose(2, 1, 0)
    (few,) = call(
        ask_kernel,
        [sds(2 * blocks + 3 * height, width, dtype=BF16)],
        [ANY, ANY],
        [
            pltpu.VMEM((blocks, 16, width), BF16),
            pltpu.VMEM((2 * blocks + 3 * height, width), F32),
            pltpu.SMEM((3, 1, height), jnp.int32),
            pltpu.SemaphoreType.DMA((5,)),
        ],
        cost=1,
        limit=FULL,
    )(index, atm_flux)
    slots = [tiles // 2 + s - 1 for s in range(3)]
    part = [from_ahead(few, d) for d in slots]

    plane = sds(levels, height, width)
    first, tile, tops, bottoms = call(
        pack_kernel,
        [sds(2, height, width), sds(3, height, width)] + [sds(3, tall, width)] * 2,
        [VMEM] * 4,
        cost=2,
    )(tracers, east_speed, north_speed, level_count)

    forced, c, r0, r1, wanted = call(
        force_kernel,
        [sds(2, height, width), sds(3, height, width)]
        + [sds(3, tall, width)] * 2
        + [sds(3, width, dtype=jnp.int32)],
        [SMEM, SMEM] + [VMEM] * 9,
        [pltpu.VMEM((3, 2 * blocks, width), F32), pltpu.VMEM((8 * height, 3 * width), F32)],
        cost=1,
    )(place, index, *part, weights, level_count, first, tile, tops, bottoms)

    def exchange(c, r0, r1):
        g0, g1 = swap(r0, "rows", rows0), swap(r1, "rows", rows1)
        return swap(c, "cols", cols0), swap(c, "cols", cols1), g0, g1

    c0, c1, g0, g1 = exchange(c, r0, r1)
    coefficients = call(solver_kernel, [plane] * 7, [ANY] + [VMEM] * 4, cost=1)(
        first, east_speed, north_speed, mixing, level_count
    )
    def answers(*which):
        found = call(
            gather_kernel,
            [sds(height, fields, width, dtype=BF16)] * len(which),
            [SMEM, VMEM],
            cost=1,
        )(wanted, atm_flux)
        return [from_ahead(block, slots[2 - s]) for s, block in zip(which, found)]

    blocks2, blocks1, blocks0 = answers(0, 1, 2)
    scratch = [pltpu.VMEM((2, levels, height, width), F32)] + [pltpu.VMEM((2, tall, width), F32)] * 2
    field, d, u0, u1 = call(
        first_step_kernel,
        [sds(2, levels, height, width), sds(2, height, width)] + [sds(2, tall, width)] * 2,
        [SMEM] + [VMEM] * 16,
        scratch,
        cost=4,
    )(place, tracers, forced, *coefficients, c, c0, c1, r0, r1, g0, g1)
    d0, d1, h0, h1 = exchange(d, u0, u1)
    (ocean_flux,) = call(remap_kernel, [sds(fields, height, width)], [VMEM] * 4, cost=2)(
        blocks0, blocks1, blocks2, weights
    )
    (result,) = call(
        second_step_kernel,
        [sds(2, levels, height, width)],
        [SMEM] + [VMEM] * 22,
        scratch,
        cost=3,
    )(place, field, *coefficients, c, c0, c1, r0, r1, g0, g1, d, d0, d1, u0, u1, h0, h1)
    return (ocean_flux, result)


def solution(mesh):
    placed = (
        P(("rows", "cols"), None, None),
        P("rows", None, None, "cols"),
        P("rows", "cols", None),
        P(None, None, "rows", "cols"),
        P(None, "rows", "cols"),
        P(None, "rows", "cols"),
        P(None, "rows", "cols"),
        P("rows", "cols"),
    )
    return jax.shard_map(
        per_device,
        mesh=mesh,
        in_specs=placed,
        out_specs=(P(None, "rows", "cols"), P(None, None, "rows", "cols")),
        check_vma=False,
    )
```

```python
import functools

import jax
import jax.numpy as jnp
from jax import lax
from jax.experimental import pallas as pl
from jax.experimental.pallas import tpu as pltpu
from jax.sharding import PartitionSpec as P

F32 = jnp.float32
BF16 = jnp.bfloat16
VMEM = pl.BlockSpec(memory_space=pltpu.VMEM)
ANY = pl.BlockSpec(memory_space=pl.ANY)
SMEM = pl.BlockSpec(memory_space=pltpu.SMEM)
LIMIT = 24 * 1024 * 1024
FULL = 60 * 1024 * 1024


def lanes(shape):
    return lax.broadcasted_iota(jnp.int32, shape, len(shape) - 1)


def sublanes(shape):
    return lax.broadcasted_iota(jnp.int32, shape, len(shape) - 2)


def turn(x, shift):
    shift = shift % x.shape[-1]
    return x if shift == 0 else pltpu.roll(x, shift, x.ndim - 1)


def ask_kernel(index_hbm, atm, out, held, wide, index, sems):
    blocks, rows = held.shape[:2]
    parts = sems.shape[0] - 1
    fetch = pltpu.make_async_copy(index_hbm, index, sems.at[parts])
    fetch.start()
    share = blocks // parts
    copies = [
        pltpu.make_async_copy(
            atm.at[p * share : (p + 1) * share, :rows, :], held.at[p * share : (p + 1) * share], sems.at[p]
        )
        for p in range(parts)
    ]
    for copy in copies:
        copy.start()
    height = index.shape[2]
    fetch.wait()
    for s in range(3):
        for y in range(height):
            at = 2 * blocks + s * height + y
            b = lax.rem(index[s, 0, y], blocks).astype(F32)
            wide[at : at + 1, :] = jnp.full((1, wide.shape[1]), b, F32)
    for p in range(parts):
        copies[p].wait()
        for b in range(p * share, (p + 1) * share):
            x = held[b].astype(F32)
            for f in range(2):
                wide[b + f * blocks : b + f * blocks + 1, :] = x[f : f + 1, :]
    out[...] = wide[...].astype(BF16)


def pack_kernel(tracers, east, north, count, first, tile, tops, bottoms):
    levels, height, width = east.shape
    lane = lanes((height, width))
    depth = count[...]
    packed = [jnp.zeros((height, width), F32) for _ in range(3)]
    for k in range(levels):
        here = (lane >> 1) == k
        for t in range(2):
            x = tracers[t, k]
            packed[t] = jnp.where(here, turn(x, 2 * k + 1), packed[t])
            tops[t, k : k + 1, :] = x[height - 1 :, :]
            bottoms[t, k : k + 1, :] = x[:1, :]
        packed[2] = jnp.where(here, turn(east[k], 2 * k + 1), packed[2])
        tops[2, k : k + 1, :] = north[k, height - 1 :, :]
    for t in range(2):
        first[t] = tracers[t, 0]
        tile[t] = packed[t]
    spare = tops.shape[1] - levels
    for t in range(3):
        tops[t, levels:, :] = jnp.zeros((spare, width), F32)
    for t in range(2):
        bottoms[t, levels:, :] = jnp.zeros((spare, width), F32)
    even = (lane & 1) == 0
    wet_last = jnp.where((lane >> 1) < depth[:, width - 1 :], 1.0, 0.0)
    wet_first = jnp.where((lane >> 1) < depth[:, :1], 1.0, 0.0)
    tile[2] = jnp.where(even, packed[2] * wet_last, wet_first)
    tall = sublanes(tops.shape[1:])
    tops[2] = tops[2] * jnp.where(tall < depth[height - 1 :, :], 1.0, 0.0)
    bottoms[2] = jnp.where(tall < depth[:1, :], 1.0, 0.0)


def solver_kernel(after, east, north, mixing, count, face_e, face_w, face_n, face_s, inv, low, ratio):
    levels, height, width = east.shape
    lane, row = lanes((height, width)), sublanes((height, width))
    depth = count[...]
    depth_e = jnp.where(lane == width - 1, levels, turn(depth, -1))
    depth_n = jnp.where(row == height - 1, levels, pltpu.roll(depth, height - 1, 0))
    depth_e = jnp.minimum(depth, depth_e)
    depth_n = jnp.minimum(depth, depth_n)
    a_prev = r_prev = jnp.zeros((height, width), F32)
    for k in range(levels):
        ce = jnp.where(depth_e > k, east[k], 0.0)
        cn = jnp.where(depth_n > k, north[k], 0.0)
        face_e[k] = ce
        face_w[k] = turn(ce, 1)
        face_n[k] = cn
        face_s[k] = pltpu.roll(cn, 1, 0)
        a = jnp.where(depth > k + 1, mixing[k], 0.0) if k + 1 < levels else jnp.zeros((height, width), F32)
        iv = 1.0 / (1.0 + a_prev + a - a_prev * r_prev)
        inv[k] = iv
        low[k] = a_prev * iv
        r_prev = a * iv
        ratio[k] = r_prev
        a_prev = a


def force_kernel(
    place, index, a0, a1, a2, weights, count, first, tile, tops, bottoms,
    forced, sent, out_r0, out_r1, wanted, held, picked,
):
    height, width = count.shape
    blocks = held.shape[1] // 2
    for s, a in enumerate((a0, a1, a2)):
        held[s] = a[: 2 * blocks].astype(F32)
        start = 2 * blocks + (2 - s) * height
        asked = a[start : start + height].astype(F32)
        own = lanes((height, width)) == sublanes((height, width))
        wanted[s : s + 1, :] = jnp.sum(jnp.where(own, asked, 0.0), 0, keepdims=True).astype(jnp.int32)
    for y in range(height):
        for s in range(3):
            b = lax.rem(index[s, 0, y], blocks)
            for f in range(2):
                picked[8 * y + f : 8 * y + f + 1, s * 128 : (s + 1) * 128] = held[
                    s, pl.ds(b + f * blocks, 1), :
                ]
    wet = jnp.where(count[...] > 0, 0.5, 0.0)
    for y in range(height):
        got = jnp.dot(
            picked[8 * y : 8 * y + 8].astype(BF16), weights[y], preferred_element_type=F32
        )
        for f in range(2):
            forced[f, y : y + 1, :] = got[f : f + 1, :]
    here = lanes((height, width)) < 2
    even = place[0] == 0
    out_r0[...] = jnp.where(even, tops[...], bottoms[...])
    out_r1[...] = jnp.where(even, bottoms[...], tops[...])
    sent[2] = tile[2]
    for t in range(2):
        x = first[t] + wet * forced[t]
        forced[t] = x
        sent[t] = jnp.where(here, turn(x, 1), tile[t])
        top, bottom = x[height - 1 :, :], x[:1, :]
        out_r0[t, :1, :] = jnp.where(even, top, bottom)
        out_r1[t, :1, :] = jnp.where(even, bottom, top)


def step(place, field, level0, face_e, face_w, face_n, face_s, inv, low, ratio,
         own_c, got_c, own_r, got_r, coef_c, coef_r, solved, edge_n, edge_s, out, messages):
    levels, height, width = face_e.shape
    lane, row = lanes((height, width)), sublanes((height, width))
    even_r, even_c = place[0] == 0, place[1] == 0
    even = (lane & 1) == 0

    def facing(own, pair):
        a, b = pair
        from_e, from_w = jnp.where(even_c, a, b), jnp.where(even_c, b, a)
        theirs = jnp.where(even, from_w, from_e)
        mine = jnp.where(even, turn(own, -1), turn(own, 1))
        return theirs, mine

    c_theirs, c_mine = facing(*coef_c)
    c = c_theirs * c_mine
    edges = []
    for t in range(2):
        theirs, mine = facing(own_c[t], (got_c[0][t], got_c[1][t]))
        flux = c * jnp.where((c > 0) == even, theirs, mine)
        edges.append(jnp.where(even, flux, turn(flux, -2)))

    def row_pair(a, b):
        return jnp.where(even_r, a, b), jnp.where(even_r, b, a)

    own_n, own_s = row_pair(coef_r[0][...], coef_r[1][...])
    from_n, from_s = row_pair(coef_r[2][...], coef_r[3][...])
    cn_row, cs_row = own_n * from_n, own_s * from_s
    for t in range(2):
        own_n, own_s = row_pair(own_r[0][t], own_r[1][t])
        from_n, from_s = row_pair(got_r[0][t], got_r[1][t])
        edge_n[t] = cn_row * jnp.where(cn_row > 0, own_n, from_n)
        edge_s[t] = cs_row * jnp.where(cs_row > 0, from_s, own_s)

    east_end, west_end = lane == width - 1, lane == 0
    north_end, south_end = row == height - 1, row == 0
    value = [None, None]
    for k in range(levels):
        ce, cw, cn, cs = face_e[k], face_w[k], face_n[k], face_s[k]
        for t in range(2):
            x = level0[t] if (k == 0 and level0 is not None) else field[t, k]
            edge = turn(edges[t], -2 * k)
            fe = jnp.where(east_end, edge, ce * jnp.where(ce > 0, x, turn(x, -1)))
            fw = jnp.where(west_end, edge, cw * jnp.where(cw > 0, turn(x, 1), x))
            fn = cn * jnp.where(cn > 0, x, pltpu.roll(x, height - 1, 0))
            fn = jnp.where(north_end, edge_n[t, k : k + 1, :], fn)
            fs = cs * jnp.where(cs > 0, pltpu.roll(x, 1, 0), x)
            fs = jnp.where(south_end, edge_s[t, k : k + 1, :], fs)
            now = (x - (fe - fw) - (fn - fs)) * inv[k]
            if k:
                now = now + low[k] * value[t]
            value[t] = now
            solved[t, k] = now
    packed = [jnp.zeros((height, width), F32)] * 2
    for k in range(levels - 1, -1, -1):
        for t in range(2):
            if k < levels - 1:
                value[t] = solved[t, k] + ratio[k] * value[t]
            y = value[t]
            out[t, k] = y
            if messages is not None:
                packed[t] = jnp.where((lane >> 1) == k, turn(y, 2 * k + 1), packed[t])
                top, bottom = y[height - 1 :, :], y[:1, :]
                messages[1][t, k : k + 1, :] = jnp.where(even_r, top, bottom)
                messages[2][t, k : k + 1, :] = jnp.where(even_r, bottom, top)
    if messages is not None:
        spare = messages[1].shape[1] - levels
        for t in range(2):
            messages[0][t] = packed[t]
            messages[1][t, levels:, :] = jnp.zeros((spare, width), F32)
            messages[2][t, levels:, :] = jnp.zeros((spare, width), F32)


def first_step_kernel(
    place, tracers, forced, face_e, face_w, face_n, face_s, inv, low, ratio,
    c, c0, c1, r0, r1, g0, g1, out, out_c, out_r0, out_r1, solved, edge_n, edge_s,
):
    step(place, tracers, forced, face_e, face_w, face_n, face_s, inv, low, ratio,
         c, (c0, c1), (r0, r1), (g0, g1), (c[2], (c0[2], c1[2])),
         (r0.at[2], r1.at[2], g0.at[2], g1.at[2]), solved, edge_n, edge_s, out, (out_c, out_r0, out_r1))


def second_step_kernel(
    place, field, face_e, face_w, face_n, face_s, inv, low, ratio,
    c, c0, c1, r0, r1, g0, g1, d, d0, d1, u0, u1, h0, h1, out, solved, edge_n, edge_s,
):
    step(place, field, None, face_e, face_w, face_n, face_s, inv, low, ratio,
         d, (d0, d1), (u0, u1), (h0, h1), (c[2], (c0[2], c1[2])),
         (r0.at[2], r1.at[2], g0.at[2], g1.at[2]), solved, edge_n, edge_s, out, None)


def gather_kernel(which, after, wanted, atm, *outs):
    for s, out in zip(which, outs):
        for y in range(out.shape[0]):
            out[y] = atm[wanted[s, y]]


def outer_kernel(a0, a2, weights, out):
    for y in range(out.shape[1]):
        got = jnp.dot(a0[y], weights[y, :128], preferred_element_type=F32)
        out[:, y, :] = got + jnp.dot(a2[y], weights[y, 256:], preferred_element_type=F32)


def inner_kernel(outer, a1, weights, out):
    for y in range(out.shape[1]):
        got = jnp.dot(a1[y], weights[y, 128:256], preferred_element_type=F32)
        out[:, y, :] = outer[:, y, :] + got


def call(kernel, outs, specs, scratch=(), cost=1, limit=LIMIT):
    return pl.pallas_call(
        kernel,
        out_shape=outs,
        in_specs=specs,
        out_specs=[VMEM] * len(outs),
        scratch_shapes=list(scratch),
        compiler_params=pltpu.CompilerParams(vmem_limit_bytes=limit),
        cost_estimate=pl.CostEstimate(flops=cost * 2000000000, bytes_accessed=cost * 3000000, transcendentals=0),
    )


def swap(block, axis, pairs):
    return lax.ppermute(block, axis, [(a, b) for a, b in pairs] + [(b, a) for a, b in pairs])


def per_device(
    atm_flux, remap_weights, intersection, tracers, east_speed, north_speed, mixing, level_count
):
    tiles, groups = lax.axis_size("cols"), lax.axis_size("rows")
    levels, height, width = east_speed.shape
    tall = -(-levels // 8) * 8
    sds = lambda *shape, dtype=F32: jax.ShapeDtypeStruct(shape, dtype)

    def from_ahead(block, distance):
        return lax.ppermute(block, "cols", [((i + distance) % tiles, i) for i in range(tiles)])

    cols0 = [(i, i + 1) for i in range(0, tiles, 2)]
    cols1 = [(i, (i + 1) % tiles) for i in range(1, tiles, 2)]
    rows0 = [(i, i + 1) for i in range(0, groups - 1, 2)]
    rows1 = [(i, i + 1) for i in range(1, groups - 1, 2)]

    place = jnp.stack([lax.axis_index("rows") % 2, lax.axis_index("cols") % 2]).astype(jnp.int32)
    weights = remap_weights.reshape(height, -1, width)

    blocks, fields = atm_flux.shape[:2]
    index = intersection.transpose(2, 1, 0)
    (few,) = call(
        ask_kernel,
        [sds(2 * blocks + 3 * height, width, dtype=BF16)],
        [ANY, ANY],
        [
            pltpu.VMEM((blocks, 16, width), BF16),
            pltpu.VMEM((2 * blocks + 3 * height, width), F32),
            pltpu.SMEM((3, 1, height), jnp.int32),
            pltpu.SemaphoreType.DMA((5,)),
        ],
        cost=1,
        limit=FULL,
    )(index, atm_flux)
    slots = [tiles // 2 + s - 1 for s in range(3)]
    part = [from_ahead(few, d) for d in slots]

    plane = sds(levels, height, width)
    first, tile, tops, bottoms = call(
        pack_kernel,
        [sds(2, height, width), sds(3, height, width)] + [sds(3, tall, width)] * 2,
        [VMEM] * 4,
        cost=2,
    )(tracers, east_speed, north_speed, level_count)

    forced, c, r0, r1, wanted = call(
        force_kernel,
        [sds(2, height, width), sds(3, height, width)]
        + [sds(3, tall, width)] * 2
        + [sds(3, width, dtype=jnp.int32)],
        [SMEM, SMEM] + [VMEM] * 9,
        [pltpu.VMEM((3, 2 * blocks, width), F32), pltpu.VMEM((8 * height, 3 * width), F32)],
        cost=1,
    )(place, index, *part, weights, level_count, first, tile, tops, bottoms)

    def exchange(c, r0, r1):
        g0, g1 = swap(r0, "rows", rows0), swap(r1, "rows", rows1)
        return swap(c, "cols", cols0), swap(c, "cols", cols1), g0, g1

    c0, c1, g0, g1 = exchange(c, r0, r1)
    coefficients = call(solver_kernel, [plane] * 7, [ANY] + [VMEM] * 4, cost=1)(
        first, east_speed, north_speed, mixing, level_count
    )
    def answers(after, *which):
        found = call(
            functools.partial(gather_kernel, which),
            [sds(height, fields, width, dtype=BF16)] * len(which),
            [ANY, SMEM, VMEM],
            cost=1,
        )(after, wanted, atm_flux)
        return [from_ahead(block, slots[2 - s]) for s, block in zip(which, found)]

    blocks2, blocks0 = answers(c, 0, 2)
    scratch = [pltpu.VMEM((2, levels, height, width), F32)] + [pltpu.VMEM((2, tall, width), F32)] * 2
    field, d, u0, u1 = call(
        first_step_kernel,
        [sds(2, levels, height, width), sds(2, height, width)] + [sds(2, tall, width)] * 2,
        [SMEM] + [VMEM] * 16,
        scratch,
        cost=4,
    )(place, tracers, forced, *coefficients, c, c0, c1, r0, r1, g0, g1)
    d0, d1, h0, h1 = exchange(d, u0, u1)
    (outer,) = call(outer_kernel, [sds(fields, height, width)], [VMEM] * 3, cost=1)(
        blocks0, blocks2, weights
    )
    (blocks1,) = answers(d, 1)
    (result,) = call(
        second_step_kernel,
        [sds(2, levels, height, width)],
        [SMEM] + [VMEM] * 22,
        scratch,
        cost=3,
    )(place, field, *coefficients, c, c0, c1, r0, r1, g0, g1, d, d0, d1, u0, u1, h0, h1)
    (ocean_flux,) = call(inner_kernel, [sds(fields, height, width)], [VMEM] * 3, cost=1)(
        outer, blocks1, weights
    )
    return (ocean_flux, result)


def solution(mesh):
    placed = (
        P(("rows", "cols"), None, None),
        P("rows", None, None, "cols"),
        P("rows", "cols", None),
        P(None, None, "rows", "cols"),
        P(None, "rows", "cols"),
        P(None, "rows", "cols"),
        P(None, "rows", "cols"),
        P("rows", "cols"),
    )
    return jax.shard_map(
        per_device,
        mesh=mesh,
        in_specs=placed,
        out_specs=(P(None, "rows", "cols"), P(None, None, "rows", "cols")),
        check_vma=False,
    )
```
